256 devices in a mesh: ta: 8 (over z), gz: 4 (over y), xy: 8 (over x, core).
Axes of the slice: x: 4, y: 4, z: 8, core: 2. Of those that a mesh axis runs over, the one named last changes fastest.
Arguments:
- right_side: float32 [2, 4, 3, 32, 16, 1024], P(None, None, None, 'ta', 'gz', 'xy'), may hold values from -6 to 6
- links: bfloat16 [4, 2, 3, 3, 32, 16, 1024], P(None, None, None, None, 'ta', 'gz', 'xy'), may hold values from -3.5 to 3.5
- clover_inverse: bfloat16 [2, 2, 6, 6, 32, 16, 1024], P(None, None, None, None, 'ta', 'gz', 'xy'), may hold values from -0.296875 to 1
- near_null: bfloat16 [8, 4, 8, 16, 12, 2, 4, 3, 256], P('ta', 'gz', 'xy'), may hold values from -6 to 6
- owners: int32 [8, 4, 8, 8], P('ta', 'gz', 'xy'), may hold values from 0 to 7, as said below
Outputs:
- smoothed: float32 [2, 4, 3, 32, 16, 1024], P(None, None, None, 'ta', 'gz', 'xy')
- coarse: float32 [8, 4, 8, 16, 2, 2, 12], P('ta', 'gz', 'xy')
The draws below stay inside these ranges and needn't reach their ends.
Inputs may be any that keep to these rules, and one draw needn't show every extreme that they name: `owners`: each device assigns at most 2 of its aggregates to any one owner; in every group of devices that share ta and gz, one owner receives exactly 2 aggregates from every device of the group.
All inputs are finite; a program needn't handle non-finite values.
Results may differ from the reference program's by a relative error of at most 0.0029.
Values may be sent and summed in bfloat16 or wider, within the bound.
A program may use at most 256 MiB of HBM per device.

```python
import jax
import jax.numpy as jnp
import numpy as np
from jax import lax

LT = 4
LZ = 4
LX = 4
LY = 32
AG = 4
NV = 12
SWEEPS = 3
NT = 32
NZ = 16
NXY = 1024
AGG_DEV = 8
AGG_SITES = 256
MOST = 2
SLOTS = 16
N_TA = 8
N_GZ = 4
N_XY = 8


def draw_clover_inverse(key, part):
    first_key, second_key = jax.random.split(jax.random.fold_in(key, 3))
    extent = (2, 2, 6, 6, NT, NZ, NXY)
    offdiag = jnp.clip(0.07 * jax.random.normal(first_key, extent, jnp.float32), -0.296875, 0.296875)
    diagonal = jax.random.uniform(second_key, (2, 6, NT, NZ, NXY), jnp.float32, 0.6, 1.0)
    identity = jnp.eye(6, dtype=jnp.float32)[:, :, None, None, None]
    real_block = offdiag[:, 0] * (1.0 - identity) + diagonal[:, :, None] * identity
    imaginary_block = offdiag[:, 1]
    return jnp.stack([real_block, imaginary_block], axis=1).astype(jnp.bfloat16)


def draw_owners(key, part):
    count = N_TA * N_GZ * N_XY
    hottest = jax.random.randint(jax.random.fold_in(key, 7), (N_TA, N_GZ), 0, N_XY, dtype=jnp.int32)
    hot_blocks = jnp.repeat(hottest.reshape(-1), N_XY)
    block_keys = jax.random.split(jax.random.fold_in(key, 11), count)

    def one_block(block_key, hot_owner):
        pool_key, order_key = jax.random.split(block_key)
        others = jnp.arange((N_XY - 1) * MOST, dtype=jnp.int32) // MOST
        others = others + (others >= hot_owner).astype(jnp.int32)
        others = jax.random.permutation(pool_key, others)[:AGG_DEV - MOST]
        listing = jnp.concatenate([jnp.full((MOST,), hot_owner, jnp.int32), others])
        return jax.random.permutation(order_key, listing)
    return jax.vmap(one_block)(block_keys, hot_blocks).reshape((N_TA, N_GZ, N_XY, AGG_DEV)).astype(jnp.int32)


def level_of(own_key, shape, shards, least, largest):
    def one(axis_at, shards_of):
        steps = jax.random.uniform(jax.random.fold_in(jax.random.fold_in(own_key, 6), axis_at), (shards_of,), jnp.float32, least / len(shards), largest / len(shards))
        return jnp.repeat(jnp.exp(steps), shape[axis_at] // shards_of).reshape((-1,) + (1,) * (len(shape) - axis_at - 1))

    factor_of = one(*shards[0])
    for cut in shards[1:]:
        factor_of = factor_of * one(*cut)
    return factor_of


def noise(key, shape, scale, limit, cuts=(), kind=jnp.bfloat16):
    drawn = scale * jax.random.normal(key, shape, jnp.float32)
    if cuts:
        drawn = drawn * level_of(key, shape, cuts, -0.22, 0.18)
    return jnp.clip(drawn, -limit, limit).astype(kind)


def setup_inputs(seed: int = 0) -> dict:
    splits = jax.random.split(jax.random.key(seed), 6)
    right_side = noise(splits[0], (2, 4, 3, NT, NZ, NXY), 1.0, 6.0, ((3, 8), (4, 4), (5, 8)), jnp.float32)
    links = noise(splits[1], (4, 2, 3, 3, NT, NZ, NXY), 3 ** -0.5, 3.5, ((4, 8), (5, 4), (6, 8)))
    clover_inverse = draw_clover_inverse(jax.random.fold_in(splits[5], 71), 0)
    near_null = noise(splits[3], (N_TA, N_GZ, N_XY, SLOTS, NV, 2, 4, 3, AGG_SITES), 0.5, 6.0, ((0, 8), (1, 4), (2, 8)))
    owners = draw_owners(jax.random.fold_in(splits[5], 71), 0)
    return {"right_side": right_side, "links": links, "clover_inverse": clover_inverse, "near_null": near_null, "owners": owners}


hopping = 0.13


def gamma_tables():
    pauli_real = np.array([[[0, 1], [1, 0]], [[0, 0], [0, 0]], [[1, 0], [0, -1]]], np.float32)
    pauli_imaginary = np.array([[[0, 0], [0, 0]], [[0, -1], [1, 0]], [[0, 0], [0, 0]]], np.float32)
    table_real = np.zeros((4, 4, 4), np.float32)
    table_imaginary = np.zeros((4, 4, 4), np.float32)
    for index in range(3):
        table_real[index, 0:2, 2:4] = pauli_imaginary[index]
        table_imaginary[index, 0:2, 2:4] = -pauli_real[index]
        table_real[index, 2:4, 0:2] = -pauli_imaginary[index]
        table_imaginary[index, 2:4, 0:2] = pauli_real[index]
    table_real[3, 0:2, 2:4] = np.eye(2, dtype=np.float32)
    table_real[3, 2:4, 0:2] = np.eye(2, dtype=np.float32)
    return table_real, table_imaginary


def spin_project(field, direction, factor):
    table_real, table_imaginary = gamma_tables()
    matrix_real = jnp.asarray(table_real[direction])
    matrix_imaginary = jnp.asarray(table_imaginary[direction])

    def spin_multiply(matrix, component):
        return jnp.tensordot(matrix, component, axes=1, precision=lax.Precision.HIGHEST)

    out_real = spin_multiply(matrix_real, field[0]) - spin_multiply(matrix_imaginary, field[1])
    out_imaginary = spin_multiply(matrix_real, field[1]) + spin_multiply(matrix_imaginary, field[0])
    return field + factor * jnp.stack([out_real, out_imaginary])


def color_apply(link, field, adjoint):
    link_real = link[0].astype(jnp.float32)
    link_imaginary = link[1].astype(jnp.float32)
    if adjoint:
        link_real = jnp.swapaxes(link_real, 0, 1)
        link_imaginary = -jnp.swapaxes(link_imaginary, 0, 1)
    field_real = field[0][:, None]
    field_imaginary = field[1][:, None]
    out_real = jnp.sum(link_real[None] * field_real - link_imaginary[None] * field_imaginary, axis=2)
    out_imaginary = jnp.sum(link_real[None] * field_imaginary + link_imaginary[None] * field_real, axis=2)
    return jnp.stack([out_real, out_imaginary])


def shift_rows(field, offset):
    extent = field.shape
    folded = field.reshape(extent[:-1] + (extent[-1] // LY, LY))
    return jnp.roll(folded, offset, axis=-1).reshape(extent)


def apply_block(clover, field):
    extent = field.shape
    vector = field.reshape((2, 2, 6) + extent[3:])
    matrix_real = clover[:, 0].astype(jnp.float32)
    matrix_imaginary = clover[:, 1].astype(jnp.float32)
    vector_real = vector[0][:, None]
    vector_imaginary = vector[1][:, None]
    out_real = jnp.sum(matrix_real * vector_real - matrix_imaginary * vector_imaginary, axis=2)
    out_imaginary = jnp.sum(matrix_real * vector_imaginary + matrix_imaginary * vector_real, axis=2)
    return jnp.stack([out_real, out_imaginary]).reshape(extent)


def dslash(field, links):
    carry_width = color_apply(links[0], field, True)
    carry_height = color_apply(links[1], field, True)
    carry_depth = color_apply(links[2], field, True)
    carry_time = color_apply(links[3], field, True)
    pairs = [
        (jnp.roll(field, -LY, axis=5), jnp.roll(carry_width, LY, axis=5)),
        (shift_rows(field, -1), shift_rows(carry_height, 1)),
        (jnp.roll(field, -1, axis=4), jnp.roll(carry_depth, 1, axis=4)),
        (jnp.roll(field, -1, axis=3), jnp.roll(carry_time, 1, axis=3)),
    ]
    summed = jnp.zeros(field.shape, jnp.float32)
    for direction in range(4):
        ahead, behind = pairs[direction]
        summed = summed + spin_project(color_apply(links[direction], ahead, False), direction, -1.0) + spin_project(behind, direction, 1.0)
    return summed


def project_group(operands):
    vectors, arrived = operands
    vectors = vectors.astype(jnp.float32).reshape(vectors.shape[:4] + (2, 2, -1))
    arrived = arrived.astype(jnp.float32).reshape(arrived.shape[:3] + (2, 2, -1))

    def contract(vector_part, tile_part):
        return jnp.einsum("jksvcx,jkscx->jkscv", vector_part, tile_part, precision=lax.Precision.HIGHEST)

    coarse_real = contract(vectors[:, :, :, :, 0], arrived[:, :, :, 0]) + contract(vectors[:, :, :, :, 1], arrived[:, :, :, 1])
    coarse_imaginary = contract(vectors[:, :, :, :, 0], arrived[:, :, :, 1]) - contract(vectors[:, :, :, :, 1], arrived[:, :, :, 0])
    return jnp.stack([coarse_real, coarse_imaginary], axis=4)


def reference(right_side, links, clover_inverse, near_null, owners):
    smoothed = apply_block(clover_inverse, right_side)
    previous = jnp.zeros(right_side.shape, jnp.float32)
    residual = previous
    for sweep in range(SWEEPS):
        hopped = dslash(smoothed, links)
        if sweep + 1 < SWEEPS:
            previous = hopped
            smoothed = apply_block(clover_inverse, right_side + hopping * hopped)
        else:
            residual = hopping * (hopped - previous)
    flat = residual.reshape((24, N_TA, LT // AG, AG, N_GZ, LZ // AG, AG, N_XY, LX // AG, AG, LY // AG, AG))
    blocks = jnp.transpose(flat, (1, 4, 7, 2, 5, 8, 10, 0, 3, 6, 9, 11))
    blocks = blocks.reshape((N_TA, N_GZ, N_XY, AGG_DEV, 24 * AGG_SITES)).astype(jnp.bfloat16)
    order = jnp.arange(AGG_DEV, dtype=jnp.int32)
    earlier = (owners[..., :, None] == owners[..., None, :]) & (order[None, :] < order[:, None])
    ranks = jnp.sum(earlier.astype(jnp.int32), axis=-1)
    target = owners * MOST + ranks
    placing = (target[..., None, :] == jnp.arange(SLOTS, dtype=jnp.int32)[:, None]).astype(jnp.float32)
    outgoing = jnp.einsum("ijksa,ijkax->ijksx", placing, blocks.astype(jnp.float32), precision=lax.Precision.HIGHEST).astype(jnp.bfloat16)
    moved = outgoing.reshape((N_TA, N_GZ, N_XY, N_XY, MOST, 24 * AGG_SITES))
    moved = jnp.transpose(moved, (0, 1, 3, 2, 4, 5)).reshape((N_TA, N_GZ, N_XY, SLOTS, 24 * AGG_SITES))
    coarse = lax.map(project_group, (near_null, moved))
    return smoothed, coarse
```

```python
import jax
import jax.numpy as jnp
from jax import lax
from jax.experimental import pallas as pl
from jax.experimental.pallas import tpu as pltpu
from jax.sharding import PartitionSpec as P

LY = 32
SWEEPS = 3
MOST = 2
AGGS = 8
NV = 12
HOPPING = 0.13
F32 = jnp.float32
BF16 = jnp.bfloat16
MESH = pl.DeviceIdType.MESH
WIDTH, HEIGHT, DEPTH, TIME = range(4)
CROSSING = ((TIME, "ta"), (DEPTH, "gz"), (WIDTH, "xy"))
UPPER = {
    WIDTH: ((1, 3), (0, 3)),
    HEIGHT: ((1, 2), (0, 0)),
    DEPTH: ((0, 3), (1, 1)),
    TIME: ((0, 0), (1, 0)),
}
LOWER = {
    WIDTH: ((1, 1), (0, 1)),
    HEIGHT: ((1, 0), (0, 2)),
    DEPTH: ((0, 1), (1, 3)),
    TIME: ((0, 0), (1, 0)),
}


def roll(value, shift, axis):
    size = value.shape[axis]
    shift = shift % size
    return value if shift == 0 else pltpu.roll(value, shift, axis)


def add_phase(base, pair, power, sign):
    if sign < 0:
        power = power + 2
    real, imaginary = pair
    turned = ((real, 1), (imaginary, 1)), ((imaginary, -1), (real, 1)), ((real, -1), (imaginary, -1)), ((imaginary, 1), (real, -1))
    out = []
    for part, (value, factor) in zip(base, turned[power % 4]):
        out.append(part + value if factor > 0 else part - value)
    return tuple(out)


def project(load, mu, sign):
    half = []
    for spin in range(2):
        source, power = UPPER[mu][spin]
        half.append([
            add_phase(load(spin, color), load(2 + source, color), power, sign)
            for color in range(3)
        ])
    return half


def color_row(link, vector, row, adjoint):
    real = imaginary = None
    for column in range(3):
        at = (column, row) if adjoint else (row, column)
        link_real, link_imaginary = link(0, *at), link(1, *at)
        vector_real, vector_imaginary = vector[column]
        first, second = link_real * vector_real, link_real * vector_imaginary
        third, fourth = link_imaginary * vector_imaginary, link_imaginary * vector_real
        if adjoint:
            first, second = first + third, second - fourth
        else:
            first, second = first - third, second + fourth
        real = first if real is None else real + first
        imaginary = second if imaginary is None else imaginary + second
    return real, imaginary


def kernel(rs_hbm, links_hbm, clover_hbm, near_hbm, owners, smoothed_hbm, coarse,
           rs, links16, clover, near, links, face_links, field, smooth, acc,
           outbox, inbox, tiles, placing, parcels, arrived, sums,
           load_sem, store_sem, send_sem, recv_sem, parcel_send, parcel_recv):
    groups = lax.axis_size("xy")
    slots = groups * MOST
    me = {axis: lax.axis_index(axis) for axis in ("ta", "gz", "xy")}

    def shifted(axis, offset):
        size = lax.axis_size(axis)
        return lax.rem(me[axis] + (offset + size), size)

    loads = [
        pltpu.make_async_copy(source, target, load_sem.at[i])
        for i, (source, target) in enumerate(
            ((rs_hbm, rs), (clover_hbm, clover), (links_hbm, links16), (near_hbm, near))
        )
    ]
    for copy in loads:
        copy.start()

    barrier = pltpu.get_barrier_semaphore()
    greeted = 0
    for axis in ("ta", "gz"):
        for offset in (1, -1):
            pl.semaphore_signal(barrier, inc=1, device_id={axis: shifted(axis, offset)}, device_id_type=MESH)
            greeted += 1
    for offset in range(1, groups):
        pl.semaphore_signal(barrier, inc=1, device_id={"xy": shifted("xy", offset)}, device_id_type=MESH)
        greeted += 1

    row8 = lax.broadcasted_iota(jnp.int32, (8, 128), 0)
    lane8 = lax.broadcasted_iota(jnp.int32, (8, 128), 1)
    upper_rows = row8 >= 4
    depth_at = row8 % 4
    width_at = lane8 // LY
    height_at = lane8 % LY

    def pack(values, mu, high):
        if mu == TIME:
            if high:
                return jnp.where(upper_rows, values[1][1], roll(values[0][1], 4, 0))
            return jnp.where(upper_rows, roll(values[1][0], 4, 0), values[0][0])
        axis, unit, at = (0, 1, depth_at) if mu == DEPTH else (1, LY, width_at)
        face = 3 if high else 0
        out = None
        for index in range(4):
            piece = roll(values[index // 2][index % 2], (index - face) * unit, axis)
            out = piece if out is None else jnp.where(at == index, piece, out)
        return out

    def unpack(packed, mu, high):
        if mu == TIME:
            if high:
                return [
                    (None, jnp.where(upper_rows, roll(packed, 4 * (1 - spin), 0), 0.0))
                    for spin in range(2)
                ]
            return [
                (jnp.where(upper_rows, 0.0, roll(packed, 4 * spin, 0)), None)
                for spin in range(2)
            ]
        axis, unit, at = (0, 1, depth_at) if mu == DEPTH else (1, LY, width_at)
        face = 3 if high else 0
        pieces = [
            jnp.where(at == face, roll(packed, (face - index) * unit, axis), 0.0)
            for index in range(4)
        ]
        return [(pieces[2 * spin], pieces[2 * spin + 1]) for spin in range(2)]

    def neighbour(value, mu, ahead):
        if mu == HEIGHT:
            step = -1 if ahead else 1
            edge = height_at == (LY - 1 if ahead else 0)
            return jnp.where(edge[None], roll(value, -step * (LY - 1), 2), roll(value, step, 2))
        if mu == TIME:
            turned = roll(value, 4, 1)
            if ahead:
                first = jnp.where(upper_rows, turned[1], turned[0])
                second = jnp.where(upper_rows, 0.0, turned[1])
            else:
                first = jnp.where(upper_rows, turned[0], 0.0)
                second = jnp.where(upper_rows, turned[1], turned[0])
            return jnp.stack([first, second])
        axis, unit, at = (1, 1, depth_at) if mu == DEPTH else (2, LY, width_at)
        edge = at == (3 if ahead else 0)
        return jnp.where(edge[None], 0.0, roll(value, -unit if ahead else unit, axis))

    def component(part, spin, color):
        return (part * 4 + spin) * 3 + color

    def load_field(spin, color):
        return field[component(0, spin, color)], field[component(1, spin, color)]

    def message(sweep, way, axis, offset):
        return pltpu.make_async_remote_copy(
            src_ref=outbox.at[sweep, way],
            dst_ref=inbox.at[sweep, way],
            send_sem=send_sem.at[sweep, way],
            recv_sem=recv_sem.at[sweep, way],
            device_id={axis: shifted(axis, offset)},
            device_id_type=MESH,
        )

    acc[...] = jnp.zeros(acc.shape, F32)
    smooth[...] = jnp.zeros(smooth.shape, F32)
    sums[...] = jnp.zeros(sums.shape, F32)

    owner = [owners[i] for i in range(AGGS)]
    target = []
    for i in range(AGGS):
        rank = jnp.int32(0)
        for j in range(i):
            rank = rank + jnp.where(owner[j] == owner[i], 1, 0)
        target.append(owner[i] * MOST + rank)
    lane_from = lax.broadcasted_iota(jnp.int32, (128, 128), 0)
    lane_to = lax.broadcasted_iota(jnp.int32, (128, 128), 1)
    slot_of = jnp.zeros((128, 128), jnp.int32)
    for i in range(AGGS):
        slot_of = jnp.where((lane_from // 4) % AGGS == i, target[i], slot_of)
    same_site = (lane_from // LY) * 4 + lane_from % 4 == lane_to % 16
    for part in range(slots // 8):
        placing[:, part * 128:(part + 1) * 128] = jnp.where(
            same_site & (slot_of == lane_to // 16 + part * 8), 1.0, 0.0
        ).astype(BF16)

    loads[0].wait()
    loads[1].wait()

    def body(sweep, carry):
        kept = jnp.where(sweep == SWEEPS - 1, 1.0, 0.0)
        for chirality in range(2):
            vector = [
                [rs[component(part, 2 * chirality, j)] + HOPPING * acc[component(part, 2 * chirality, j)]
                 for part in range(2)]
                for j in range(6)
            ]
            for i in range(6):
                real = imaginary = None
                for j in range(6):
                    block_real = clover[chirality, 0, i * 6 + j].astype(F32).reshape(2, 8, 128)
                    block_imaginary = clover[chirality, 1, i * 6 + j].astype(F32).reshape(2, 8, 128)
                    first = block_real * vector[j][0] - block_imaginary * vector[j][1]
                    second = block_real * vector[j][1] + block_imaginary * vector[j][0]
                    real = first if real is None else real + first
                    imaginary = second if imaginary is None else imaginary + second
                for part, value in enumerate((real, imaginary)):
                    at = component(part, 2 * chirality, i)
                    field[at] = value - kept * smooth[at]
                    smooth[at] = value

        @pl.when(sweep == SWEEPS - 1)
        def _():
            pltpu.make_async_copy(smooth, smoothed_hbm, store_sem).start()

        @pl.when(sweep == 0)
        def _():
            loads[2].wait()
            for mu in range(4):
                for part in range(2):
                    for at in range(9):
                        links[mu, part, at] = links16[mu, part, at].astype(F32).reshape(2, 8, 128)
            for order, (mu, _) in enumerate(CROSSING):
                for part in range(2):
                    for at in range(9):
                        value = links[mu, part, at]
                        face_links[order, part, at] = pack([value, value], mu, True)
            pl.semaphore_wait(barrier, greeted)

        for order, (mu, axis) in enumerate(CROSSING):
            half = project(load_field, mu, -1)
            for part in range(2):
                for color in range(3):
                    outbox[sweep, 2 * order, part * 3 + color] = pack(
                        [half[0][color][part], half[1][color][part]], mu, False)
            message(sweep, 2 * order, axis, -1).start()
        for order, (mu, axis) in enumerate(CROSSING):
            half = project(load_field, mu, 1)
            packed = [
                tuple(pack([half[0][color][part], half[1][color][part]], mu, True) for part in range(2))
                for color in range(3)
            ]

            def face_link(part, row, column, order=order):
                return face_links[order, part, row * 3 + column]

            for row in range(3):
                pair = color_row(face_link, packed, row, True)
                for part in range(2):
                    outbox[sweep, 2 * order + 1, part * 3 + row] = pair[part]
            message(sweep, 2 * order + 1, axis, 1).start()

        started = False
        for mu in (HEIGHT, TIME, DEPTH, WIDTH):
            def link(part, row, column, mu=mu):
                return links[mu, part, row * 3 + column]

            for sign in (-1, 1):
                half = project(load_field, mu, sign)
                if sign < 0:
                    half = [[tuple(neighbour(value, mu, True) for value in pair) for pair in spin] for spin in half]
                for row in range(3):
                    moved = []
                    for spin in range(2):
                        pair = color_row(link, half[spin], row, sign > 0)
                        if sign > 0:
                            pair = tuple(neighbour(value, mu, False) for value in pair)
                        moved.append(pair)
                    for spin in range(4):
                        places = [component(part, spin, row) for part in range(2)]
                        base = tuple(acc[at] for at in places) if started else (0.0, 0.0)
                        if spin < 2:
                            total = add_phase(base, moved[spin], 0, 1)
                        else:
                            source, power = LOWER[mu][spin - 2]
                            total = add_phase(base, moved[source], power, sign)
                        for at, value in zip(places, total):
                            acc[at] = value
                started = True

        for order, (mu, axis) in enumerate(CROSSING):
            message(sweep, 2 * order, axis, -1).wait_recv()
            message(sweep, 2 * order + 1, axis, 1).wait_recv()
        for row in range(3):
            totals = [
                [[acc[component(part, spin, row), side] for side in range(2)] for part in range(2)]
                for spin in range(4)
            ]
            for order, (mu, axis) in enumerate(CROSSING):
                def face_link(part, at_row, column, order=order):
                    return face_links[order, part, at_row * 3 + column]

                for sign in (-1, 1):
                    way = 2 * order + (0 if sign < 0 else 1)
                    if sign < 0:
                        packed = [
                            (inbox[sweep, way, color], inbox[sweep, way, 3 + color]) for color in range(3)
                        ]
                        pair = color_row(face_link, packed, row, False)
                    else:
                        pair = inbox[sweep, way, row], inbox[sweep, way, 3 + row]
                    spread = [unpack(value, mu, sign < 0) for value in pair]
                    for side in range(2):
                        if spread[0][0][side] is None:
                            continue
                        pieces = [(spread[0][spin][side], spread[1][spin][side]) for spin in range(2)]
                        for spin in range(4):
                            base = totals[spin][0][side], totals[spin][1][side]
                            if spin < 2:
                                total = add_phase(base, pieces[spin], 0, 1)
                            else:
                                source, power = LOWER[mu][spin - 2]
                                total = add_phase(base, pieces[source], power, sign)
                            totals[spin][0][side], totals[spin][1][side] = total
            for spin in range(4):
                for part in range(2):
                    for side in range(2):
                        acc[component(part, spin, row), side] = totals[spin][part][side]
        return carry

    lax.fori_loop(0, SWEEPS, body, 0)

    for part in range(2):
        for color in range(3):
            for spin in range(4):
                value = HOPPING * acc[component(part, spin, color)]
                for side in range(2):
                    at = ((part * 3 + color) * 2 + side) * 4 + spin
                    tiles[at * 8:(at + 1) * 8, :] = value[side]
    rows = jnp.concatenate([tiles[pl.ds(r, 48, stride=8), :] for r in range(8)], axis=0).astype(BF16)
    placed = jnp.dot(rows, placing[...], preferred_element_type=F32)
    for part in range(slots // 8):
        parts = [placed[r * 48:(r + 1) * 48, part * 128:(part + 1) * 128] for r in range(8)]
        lane = lax.broadcasted_iota(jnp.int32, (48, 128), 1) // 16
        for step in (1, 2, 4):
            for r in range(8):
                if r & step:
                    continue
                first, second = parts[r], parts[r + step]
                odd = (lane & step) != 0
                parts[r] = jnp.where(odd, roll(second, step * 16, 1), first)
                parts[r + step] = jnp.where(odd, second, roll(first, -step * 16, 1))
        for r in range(8):
            slot = part * 8 + r
            parcels[slot // MOST, slot % MOST] = parts[r].astype(BF16)

    def parcel(offset):
        return pltpu.make_async_remote_copy(
            src_ref=parcels.at[shifted("xy", offset)],
            dst_ref=arrived.at[offset],
            send_sem=parcel_send.at[offset],
            recv_sem=parcel_recv.at[offset],
            device_id={"xy": shifted("xy", offset)},
            device_id_type=MESH,
        )

    for offset in sorted(range(1, groups), key=lambda o: -min(o, groups - o)):
        parcel(offset).start()
    arrived[0] = parcels[me["xy"]]
    loads[3].wait()

    def contract(index, carry):
        half = (index + 1) // 2
        offset = jnp.where(index % 2 == 1, half, lax.rem(groups - half, groups))

        @pl.when(index > 0)
        def _():
            parcel(offset).wait_recv()

        source = lax.rem(me["xy"] - offset + groups, groups)
        for m in range(MOST):
            slot = source * MOST + m
            tile = arrived[offset, m].astype(F32).reshape(6, 8, 128)
            turned = jnp.concatenate([tile[3:], -tile[:3]], axis=0)
            for v in range(NV):
                vector = near[slot * NV + v].astype(F32).reshape(6, 8, 128)
                for part, other in enumerate((tile, turned)):
                    total = jnp.sum(jnp.sum(vector * other, axis=0), axis=1, keepdims=True)
                    sums[v * 2 + part] = jnp.where(lane8 == slot, total, sums[v * 2 + part])
        return carry

    lax.fori_loop(0, groups, contract, 0)
    total = sums[...]
    total = total + roll(total, 4, 1)
    total = total + roll(total, -1, 1)
    total = total.reshape(NV, 2, 8, 128)
    for chirality in range(2):
        coarse[chirality] = total[:, :, 2 * chirality, :slots]

    for sweep in range(SWEEPS):
        for order, (mu, axis) in enumerate(CROSSING):
            message(sweep, 2 * order, axis, -1).wait_send()
            message(sweep, 2 * order + 1, axis, 1).wait_send()
    for offset in range(1, groups):
        parcel(offset).wait_send()
    pltpu.make_async_copy(smooth, smoothed_hbm, store_sem).wait()


def shards(right_side, links, clover_inverse, near_null, owners):
    groups = lax.axis_size("xy")
    slots = groups * MOST
    near = jnp.transpose(near_null[0, 0, 0], (0, 1, 2, 4, 3, 5)).reshape(slots, NV, 2, 3, 4, 2, 128)
    near = jnp.transpose(near, (0, 1, 2, 3, 5, 4, 6)).reshape(slots * NV, 48, 128)
    anywhere = pl.BlockSpec(memory_space=pl.ANY)
    vmem = pltpu.VMEM
    smoothed, coarse = pl.pallas_call(
        kernel,
        out_shape=(
            jax.ShapeDtypeStruct((24, 2, 8, 128), F32),
            jax.ShapeDtypeStruct((2, NV, 2, slots), F32),
        ),
        in_specs=[anywhere] * 4 + [pl.BlockSpec(memory_space=pltpu.SMEM)],
        out_specs=(anywhere, pl.BlockSpec(memory_space=vmem)),
        scratch_shapes=[
            vmem((24, 2, 8, 128), F32),
            vmem((4, 2, 9, 16, 128), BF16),
            vmem((2, 2, 36, 16, 128), BF16),
            vmem((slots * NV, 48, 128), BF16),
            vmem((4, 2, 9, 2, 8, 128), F32),
            vmem((3, 2, 9, 8, 128), F32),
            vmem((24, 2, 8, 128), F32),
            vmem((24, 2, 8, 128), F32),
            vmem((24, 2, 8, 128), F32),
            vmem((SWEEPS, 6, 6, 8, 128), F32),
            vmem((SWEEPS, 6, 6, 8, 128), F32),
            vmem((384, 128), F32),
            vmem((128, slots * 16), BF16),
            vmem((groups, MOST, 48, 128), BF16),
            vmem((groups, MOST, 48, 128), BF16),
            vmem((NV * 2, 8, 128), F32),
            pltpu.SemaphoreType.DMA((4,)),
            pltpu.SemaphoreType.DMA,
            pltpu.SemaphoreType.DMA((SWEEPS, 6)),
            pltpu.SemaphoreType.DMA((SWEEPS, 6)),
            pltpu.SemaphoreType.DMA((groups,)),
            pltpu.SemaphoreType.DMA((groups,)),
        ],
        compiler_params=pltpu.CompilerParams(
            collective_id=0, has_side_effects=True, vmem_limit_bytes=62 * 1024 * 1024
        ),
        name="smooth_and_restrict",
    )(
        right_side.reshape(24, 2, 8, 128),
        links.reshape(4, 2, 9, 16, 128),
        clover_inverse.reshape(2, 2, 36, 16, 128),
        near,
        owners.reshape(-1),
    )
    coarse = jnp.transpose(coarse, (3, 0, 2, 1))[None, None, None]
    return smoothed.reshape(2, 4, 3, 4, 4, 128), coarse


def solution(mesh):
    placed = (
        P(None, None, None, "ta", "gz", "xy"),
        P(None, None, None, None, "ta", "gz", "xy"),
        P(None, None, None, None, "ta", "gz", "xy"),
        P("ta", "gz", "xy", None, None, None, None, None, None),
        P("ta", "gz", "xy", None),
    )
    return jax.shard_map(
        shards,
        mesh=mesh,
        in_specs=placed,
        out_specs=(
            P(None, None, None, "ta", "gz", "xy"),
            P("ta", "gz", "xy", None, None, None, None),
        ),
        check_vma=False,
    )
```

```python
import jax
import jax.numpy as jnp
from jax import lax
from jax.experimental import pallas as pl
from jax.experimental.pallas import tpu as pltpu
from jax.sharding import PartitionSpec as P

LY = 32
SWEEPS = 3
MOST = 2
AGGS = 8
NV = 12
HOPPING = 0.13
F32 = jnp.float32
BF16 = jnp.bfloat16
MESH = pl.DeviceIdType.MESH
WIDTH, HEIGHT, DEPTH, TIME = range(4)
CROSSING = ((TIME, "ta"), (DEPTH, "gz"), (WIDTH, "xy"))
UPPER = {
    WIDTH: ((1, 3), (0, 3)),
    HEIGHT: ((1, 2), (0, 0)),
    DEPTH: ((0, 3), (1, 1)),
    TIME: ((0, 0), (1, 0)),
}
LOWER = {
    WIDTH: ((1, 1), (0, 1)),
    HEIGHT: ((1, 0), (0, 2)),
    DEPTH: ((0, 1), (1, 3)),
    TIME: ((0, 0), (1, 0)),
}


def roll(value, shift, axis):
    size = value.shape[axis]
    shift = shift % size
    return value if shift == 0 else pltpu.roll(value, shift, axis)


def add_phase(base, pair, power, sign):
    if sign < 0:
        power = power + 2
    real, imaginary = pair
    turned = ((real, 1), (imaginary, 1)), ((imaginary, -1), (real, 1)), ((real, -1), (imaginary, -1)), ((imaginary, 1), (real, -1))
    out = []
    for part, (value, factor) in zip(base, turned[power % 4]):
        out.append(part + value if factor > 0 else part - value)
    return tuple(out)


def project(load, mu, sign):
    half = []
    for spin in range(2):
        source, power = UPPER[mu][spin]
        half.append([
            add_phase(load(spin, color), load(2 + source, color), power, sign)
            for color in range(3)
        ])
    return half


def color_row(link, vector, row, adjoint):
    real = imaginary = None
    for column in range(3):
        at = (column, row) if adjoint else (row, column)
        link_real, link_imaginary = link(0, *at), link(1, *at)
        vector_real, vector_imaginary = vector[column]
        first, second = link_real * vector_real, link_real * vector_imaginary
        third, fourth = link_imaginary * vector_imaginary, link_imaginary * vector_real
        if adjoint:
            first, second = first + third, second - fourth
        else:
            first, second = first - third, second + fourth
        real = first if real is None else real + first
        imaginary = second if imaginary is None else imaginary + second
    return real, imaginary


def kernel(rs_hbm, links_hbm, clover_hbm, near_hbm, owners_hbm, smooth, sums,
           rs, links16, clover, near, owners, links, face_links, field, acc,
           outbox, inbox, tiles, placing, parcels, arrived,
           load_sem, send_sem, recv_sem, parcel_send, parcel_recv):
    groups = lax.axis_size("xy")
    slots = groups * MOST
    me = {axis: lax.axis_index(axis) for axis in ("ta", "gz", "xy")}

    def shifted(axis, offset):
        size = lax.axis_size(axis)
        return lax.rem(me[axis] + (offset + size), size)

    loads = [
        pltpu.make_async_copy(source, target, load_sem.at[i])
        for i, (source, target) in enumerate(
            ((rs_hbm, rs), (clover_hbm, clover), (links_hbm, links16), (near_hbm, near), (owners_hbm, owners))
        )
    ]
    for copy in loads[:3] + loads[4:]:
        copy.start()

    barrier = pltpu.get_barrier_semaphore()
    greeted = 0
    for axis in ("ta", "gz"):
        for offset in (1, -1):
            pl.semaphore_signal(barrier, inc=1, device_id={axis: shifted(axis, offset)}, device_id_type=MESH)
            greeted += 1
    for offset in range(1, groups):
        pl.semaphore_signal(barrier, inc=1, device_id={"xy": shifted("xy", offset)}, device_id_type=MESH)
        greeted += 1

    row8 = lax.broadcasted_iota(jnp.int32, (8, 128), 0)
    lane8 = lax.broadcasted_iota(jnp.int32, (8, 128), 1)
    upper_rows = row8 >= 4
    depth_at = row8 % 4
    width_at = lane8 // LY
    height_at = lane8 % LY

    def pack(values, mu, high):
        if mu == TIME:
            if high:
                return jnp.where(upper_rows, values[1][1], roll(values[0][1], 4, 0))
            return jnp.where(upper_rows, roll(values[1][0], 4, 0), values[0][0])
        axis, unit, at = (0, 1, depth_at) if mu == DEPTH else (1, LY, width_at)
        face = 3 if high else 0
        out = None
        for index in range(4):
            piece = roll(values[index // 2][index % 2], (index - face) * unit, axis)
            out = piece if out is None else jnp.where(at == index, piece, out)
        return out

    def unpack(packed, mu, high):
        if mu == TIME:
            if high:
                return [
                    (None, jnp.where(upper_rows, roll(packed, 4 * (1 - spin), 0), 0.0))
                    for spin in range(2)
                ]
            return [
                (jnp.where(upper_rows, 0.0, roll(packed, 4 * spin, 0)), None)
                for spin in range(2)
            ]
        axis, unit, at = (0, 1, depth_at) if mu == DEPTH else (1, LY, width_at)
        face = 3 if high else 0
        pieces = [
            jnp.where(at == face, roll(packed, (face - index) * unit, axis), 0.0)
            for index in range(4)
        ]
        return [(pieces[2 * spin], pieces[2 * spin + 1]) for spin in range(2)]

    def neighbour(value, mu, ahead):
        if mu == HEIGHT:
            step = -1 if ahead else 1
            edge = height_at == (LY - 1 if ahead else 0)
            return jnp.where(edge[None], roll(value, -step * (LY - 1), 2), roll(value, step, 2))
        if mu == TIME:
            turned = roll(value, 4, 1)
            if ahead:
                first = jnp.where(upper_rows, turned[1], turned[0])
                second = jnp.where(upper_rows, 0.0, turned[1])
            else:
                first = jnp.where(upper_rows, turned[0], 0.0)
                second = jnp.where(upper_rows, turned[1], turned[0])
            return jnp.stack([first, second])
        axis, unit, at = (1, 1, depth_at) if mu == DEPTH else (2, LY, width_at)
        edge = at == (3 if ahead else 0)
        return jnp.where(edge[None], 0.0, roll(value, -unit if ahead else unit, axis))

    def component(part, spin, color):
        return (part * 4 + spin) * 3 + color

    def load_field(spin, color):
        return field[component(0, spin, color)], field[component(1, spin, color)]

    def message(sweep, way, axis, offset):
        return pltpu.make_async_remote_copy(
            src_ref=outbox.at[sweep, way],
            dst_ref=inbox.at[sweep, way],
            send_sem=send_sem.at[sweep, way],
            recv_sem=recv_sem.at[sweep, way],
            device_id={axis: shifted(axis, offset)},
            device_id_type=MESH,
        )

    acc[...] = jnp.zeros(acc.shape, F32)
    smooth[...] = jnp.zeros(smooth.shape, F32)
    sums[...] = jnp.zeros(sums.shape, F32)

    loads[0].wait()
    loads[1].wait()

    def body(sweep, carry):
        kept = jnp.where(sweep == SWEEPS - 1, 1.0, 0.0)
        for chirality in range(2):
            vector = [
                [rs[component(part, 2 * chirality, j)] + HOPPING * acc[component(part, 2 * chirality, j)]
                 for part in range(2)]
                for j in range(6)
            ]
            for i in range(6):
                real = imaginary = None
                for j in range(6):
                    block_real = clover[chirality, 0, i * 6 + j].astype(F32).reshape(2, 8, 128)
                    block_imaginary = clover[chirality, 1, i * 6 + j].astype(F32).reshape(2, 8, 128)
                    first = block_real * vector[j][0] - block_imaginary * vector[j][1]
                    second = block_real * vector[j][1] + block_imaginary * vector[j][0]
                    real = first if real is None else real + first
                    imaginary = second if imaginary is None else imaginary + second
                for part, value in enumerate((real, imaginary)):
                    at = component(part, 2 * chirality, i)
                    field[at] = value - kept * smooth[at]
                    smooth[at] = value

        @pl.when(sweep == 0)
        def _():
            loads[2].wait()
            for order, (mu, _) in enumerate(CROSSING):
                for part in range(2):
                    for at in range(9):
                        value = links16[mu, part, at].astype(F32).reshape(2, 8, 128)
                        face_links[order, part, at] = pack([value, value], mu, True)
            pl.semaphore_wait(barrier, greeted)

        for order, (mu, axis) in enumerate(CROSSING):
            half = project(load_field, mu, -1)
            for part in range(2):
                for color in range(3):
                    outbox[sweep, 2 * order, part * 3 + color] = pack(
                        [half[0][color][part], half[1][color][part]], mu, False)
            message(sweep, 2 * order, axis, -1).start()
        for order, (mu, axis) in enumerate(CROSSING):
            half = project(load_field, mu, 1)
            packed = [
                tuple(pack([half[0][color][part], half[1][color][part]], mu, True) for part in range(2))
                for color in range(3)
            ]

            def face_link(part, row, column, order=order):
                return face_links[order, part, row * 3 + column]

            for row in range(3):
                pair = color_row(face_link, packed, row, True)
                for part in range(2):
                    outbox[sweep, 2 * order + 1, part * 3 + row] = pair[part]
            message(sweep, 2 * order + 1, axis, 1).start()

        @pl.when(sweep == 0)
        def _():
            loads[3].start()
            loads[4].wait()
            owner = [owners[i] for i in range(AGGS)]
            target = []
            for i in range(AGGS):
                rank = jnp.int32(0)
                for j in range(i):
                    rank = rank + jnp.where(owner[j] == owner[i], 1, 0)
                target.append(owner[i] * MOST + rank)
            lane_from = lax.broadcasted_iota(jnp.int32, (128, 128), 0)
            lane_to = lax.broadcasted_iota(jnp.int32, (128, 128), 1)
            slot_of = jnp.zeros((128, 128), jnp.int32)
            for i in range(AGGS):
                slot_of = jnp.where((lane_from // 4) % AGGS == i, target[i], slot_of)
            same_site = (lane_from // LY) * 4 + lane_from % 4 == lane_to % 16
            for part in range(slots // 8):
                placing[:, part * 128:(part + 1) * 128] = jnp.where(
                    same_site & (slot_of == lane_to // 16 + part * 8), 1.0, 0.0
                ).astype(BF16)
            for mu in range(4):
                for part in range(2):
                    for at in range(9):
                        links[mu, part, at] = links16[mu, part, at].astype(F32).reshape(2, 8, 128)

        started = False
        for mu in (HEIGHT, TIME, DEPTH, WIDTH):
            def link(part, row, column, mu=mu):
                return links[mu, part, row * 3 + column]

            for sign in (-1, 1):
                half = project(load_field, mu, sign)
                if sign < 0:
                    half = [[tuple(neighbour(value, mu, True) for value in pair) for pair in spin] for spin in half]
                for row in range(3):
                    moved = []
                    for spin in range(2):
                        pair = color_row(link, half[spin], row, sign > 0)
                        if sign > 0:
                            pair = tuple(neighbour(value, mu, False) for value in pair)
                        moved.append(pair)
                    for spin in range(4):
                        places = [component(part, spin, row) for part in range(2)]
                        base = tuple(acc[at] for at in places) if started else (0.0, 0.0)
                        if spin < 2:
                            total = add_phase(base, moved[spin], 0, 1)
                        else:
                            source, power = LOWER[mu][spin - 2]
                            total = add_phase(base, moved[source], power, sign)
                        for at, value in zip(places, total):
                            acc[at] = value
                started = True

        for order, (mu, axis) in enumerate(CROSSING):
            message(sweep, 2 * order, axis, -1).wait_recv()
            message(sweep, 2 * order + 1, axis, 1).wait_recv()
        for row in range(3):
            totals = [
                [[acc[component(part, spin, row), side] for side in range(2)] for part in range(2)]
                for spin in range(4)
            ]
            for order, (mu, axis) in enumerate(CROSSING):
                def face_link(part, at_row, column, order=order):
                    return face_links[order, part, at_row * 3 + column]

                for sign in (-1, 1):
                    way = 2 * order + (0 if sign < 0 else 1)
                    if sign < 0:
                        packed = [
                            (inbox[sweep, way, color], inbox[sweep, way, 3 + color]) for color in range(3)
                        ]
                        pair = color_row(face_link, packed, row, False)
                    else:
                        pair = inbox[sweep, way, row], inbox[sweep, way, 3 + row]
                    spread = [unpack(value, mu, sign < 0) for value in pair]
                    for side in range(2):
                        if spread[0][0][side] is None:
                            continue
                        pieces = [(spread[0][spin][side], spread[1][spin][side]) for spin in range(2)]
                        for spin in range(4):
                            base = totals[spin][0][side], totals[spin][1][side]
                            if spin < 2:
                                total = add_phase(base, pieces[spin], 0, 1)
                            else:
                                source, power = LOWER[mu][spin - 2]
                                total = add_phase(base, pieces[source], power, sign)
                            totals[spin][0][side], totals[spin][1][side] = total
            for spin in range(4):
                for part in range(2):
                    for side in range(2):
                        acc[component(part, spin, row), side] = totals[spin][part][side]
        return carry

    lax.fori_loop(0, SWEEPS, body, 0)

    for part in range(2):
        for color in range(3):
            for spin in range(4):
                value = HOPPING * acc[component(part, spin, color)]
                for side in range(2):
                    at = ((part * 3 + color) * 2 + side) * 4 + spin
                    tiles[at * 8:(at + 1) * 8, :] = value[side]
    rows = jnp.concatenate([tiles[pl.ds(r, 48, stride=8), :] for r in range(8)], axis=0).astype(BF16)
    placed = jnp.dot(rows, placing[...], preferred_element_type=F32)
    for part in range(slots // 8):
        parts = [placed[r * 48:(r + 1) * 48, part * 128:(part + 1) * 128] for r in range(8)]
        lane = lax.broadcasted_iota(jnp.int32, (48, 128), 1) // 16
        for step in (1, 2, 4):
            for r in range(8):
                if r & step:
                    continue
                first, second = parts[r], parts[r + step]
                odd = (lane & step) != 0
                parts[r] = jnp.where(odd, roll(second, step * 16, 1), first)
                parts[r + step] = jnp.where(odd, second, roll(first, -step * 16, 1))
        for r in range(8):
            slot = part * 8 + r
            parcels[slot // MOST, slot % MOST] = parts[r].astype(BF16)

    def parcel(offset):
        return pltpu.make_async_remote_copy(
            src_ref=parcels.at[shifted("xy", offset)],
            dst_ref=arrived.at[offset],
            send_sem=parcel_send.at[offset],
            recv_sem=parcel_recv.at[offset],
            device_id={"xy": shifted("xy", offset)},
            device_id_type=MESH,
        )

    for offset in sorted(range(1, groups), key=lambda o: -min(o, groups - o)):
        parcel(offset).start()
    arrived[0] = parcels[me["xy"]]
    loads[3].wait()

    def contract(index, carry):
        half = (index + 1) // 2
        offset = jnp.where(index % 2 == 1, half, lax.rem(groups - half, groups))

        @pl.when(index > 0)
        def _():
            parcel(offset).wait_recv()

        source = lax.rem(me["xy"] - offset + groups, groups)
        for m in range(MOST):
            slot = source * MOST + m
            tile = arrived[offset, m].astype(F32).reshape(6, 8, 128)
            turned = jnp.concatenate([tile[3:], -tile[:3]], axis=0)
            for v in range(NV):
                vector = near[slot * NV + v].astype(F32).reshape(6, 8, 128)
                for part, other in enumerate((tile, turned)):
                    total = jnp.sum(jnp.sum(vector * other, axis=0), axis=1, keepdims=True)
                    sums[v * 2 + part] = jnp.where(lane8 == slot, total, sums[v * 2 + part])
        return carry

    lax.fori_loop(0, groups, contract, 0)
    for sweep in range(SWEEPS):
        for order, (mu, axis) in enumerate(CROSSING):
            message(sweep, 2 * order, axis, -1).wait_send()
            message(sweep, 2 * order + 1, axis, 1).wait_send()
    for offset in range(1, groups):
        parcel(offset).wait_send()


def finish(smooth, sums, smoothed, coarse, staged, sems):
    first = pltpu.make_async_copy(smooth, smoothed, sems.at[0])
    first.start()
    slots = coarse.shape[-1]
    total = sums[...]
    total = total + roll(total, 4, 1)
    total = total + roll(total, -1, 1)
    total = total.reshape(NV, 2, 8, 128)
    for chirality in range(2):
        staged[chirality] = total[:, :, 2 * chirality, :slots]
    second = pltpu.make_async_copy(staged, coarse, sems.at[1])
    second.start()
    first.wait()
    second.wait()


def shards(right_side, links, clover_inverse, near_null, owners):
    groups = lax.axis_size("xy")
    slots = groups * MOST
    near = jnp.transpose(near_null[0, 0, 0], (0, 1, 2, 4, 3, 5)).reshape(slots, NV, 2, 3, 4, 2, 128)
    near = jnp.transpose(near, (0, 1, 2, 3, 5, 4, 6)).reshape(slots * NV, 48, 128)
    anywhere = pl.BlockSpec(memory_space=pl.ANY)
    vmem = pltpu.VMEM
    inside = pl.BlockSpec(memory_space=vmem)
    operands = [
        pltpu.with_memory_space_constraint(value, pltpu.HBM)
        for value in (
            right_side.reshape(24, 2, 8, 128),
            links.reshape(4, 2, 9, 16, 128),
            clover_inverse.reshape(2, 2, 36, 16, 128),
            near,
            owners.reshape(-1),
        )
    ]
    smooth, sums = pl.pallas_call(
        kernel,
        out_shape=(vmem((24, 2, 8, 128), F32), vmem((NV * 2, 8, 128), F32)),
        in_specs=[anywhere] * 5,
        out_specs=(inside, inside),
        scratch_shapes=[
            vmem((24, 2, 8, 128), F32),
            vmem((4, 2, 9, 16, 128), BF16),
            vmem((2, 2, 36, 16, 128), BF16),
            vmem((slots * NV, 48, 128), BF16),
            pltpu.SMEM((AGGS,), jnp.int32),
            vmem((4, 2, 9, 2, 8, 128), F32),
            vmem((3, 2, 9, 8, 128), F32),
            vmem((24, 2, 8, 128), F32),
            vmem((24, 2, 8, 128), F32),
            vmem((SWEEPS, 6, 6, 8, 128), F32),
            vmem((SWEEPS, 6, 6, 8, 128), F32),
            vmem((384, 128), F32),
            vmem((128, slots * 16), BF16),
            vmem((groups, MOST, 48, 128), BF16),
            vmem((groups, MOST, 48, 128), BF16),
            pltpu.SemaphoreType.DMA((5,)),
            pltpu.SemaphoreType.DMA((SWEEPS, 6)),
            pltpu.SemaphoreType.DMA((SWEEPS, 6)),
            pltpu.SemaphoreType.DMA((groups,)),
            pltpu.SemaphoreType.DMA((groups,)),
        ],
        compiler_params=pltpu.CompilerParams(
            collective_id=0, has_side_effects=True, vmem_limit_bytes=32 * 1024 * 1024
        ),
        name="smooth_and_restrict",
    )(*operands)
    smoothed, coarse = pl.pallas_call(
        finish,
        out_shape=(
            jax.ShapeDtypeStruct((24, 2, 8, 128), F32),
            jax.ShapeDtypeStruct((2, NV, 2, slots), F32),
        ),
        in_specs=[anywhere, inside],
        out_specs=(anywhere, anywhere),
        scratch_shapes=[vmem((2, NV, 2, slots), F32), pltpu.SemaphoreType.DMA((2,))],
        compiler_params=pltpu.CompilerParams(vmem_limit_bytes=32 * 1024 * 1024),
        name="finish",
    )(smooth, sums)
    coarse = jnp.transpose(coarse, (3, 0, 2, 1))[None, None, None]
    return smoothed.reshape(2, 4, 3, 4, 4, 128), coarse


def solution(mesh):
    placed = (
        P(None, None, None, "ta", "gz", "xy"),
        P(None, None, None, None, "ta", "gz", "xy"),
        P(None, None, None, None, "ta", "gz", "xy"),
        P("ta", "gz", "xy", None, None, None, None, None, None),
        P("ta", "gz", "xy", None),
    )
    return jax.shard_map(
        shards,
        mesh=mesh,
        in_specs=placed,
        out_specs=(
            P(None, None, None, "ta", "gz", "xy"),
            P("ta", "gz", "xy", None, None, None, None),
        ),
        check_vma=False,
    )
```

```python
import jax
import jax.numpy as jnp
from jax import lax
from jax.experimental import pallas as pl
from jax.experimental.pallas import tpu as pltpu
from jax.sharding import PartitionSpec as P

LY = 32
SWEEPS = 3
MOST = 2
AGGS = 8
NV = 12
HOPPING = 0.13
F32 = jnp.float32
BF16 = jnp.bfloat16
MESH = pl.DeviceIdType.MESH
WIDTH, HEIGHT, DEPTH, TIME = range(4)
CROSSING = ((TIME, "ta"), (DEPTH, "gz"), (WIDTH, "xy"))
UPPER = {
    WIDTH: ((1, 3), (0, 3)),
    HEIGHT: ((1, 2), (0, 0)),
    DEPTH: ((0, 3), (1, 1)),
    TIME: ((0, 0), (1, 0)),
}
LOWER = {
    WIDTH: ((1, 1), (0, 1)),
    HEIGHT: ((1, 0), (0, 2)),
    DEPTH: ((0, 1), (1, 3)),
    TIME: ((0, 0), (1, 0)),
}


def roll(value, shift, axis):
    size = value.shape[axis]
    shift = shift % size
    return value if shift == 0 else pltpu.roll(value, shift, axis)


def add_phase(base, pair, power, sign):
    if sign < 0:
        power = power + 2
    real, imaginary = pair
    turned = ((real, 1), (imaginary, 1)), ((imaginary, -1), (real, 1)), ((real, -1), (imaginary, -1)), ((imaginary, 1), (real, -1))
    out = []
    for part, (value, factor) in zip(base, turned[power % 4]):
        out.append(part + value if factor > 0 else part - value)
    return tuple(out)


def project(load, mu, sign):
    half = []
    for spin in range(2):
        source, power = UPPER[mu][spin]
        half.append([
            add_phase(load(spin, color), load(2 + source, color), power, sign)
            for color in range(3)
        ])
    return half


def color_row(link, vector, row, adjoint):
    real = imaginary = None
    for column in range(3):
        at = (column, row) if adjoint else (row, column)
        link_real, link_imaginary = link(0, *at), link(1, *at)
        vector_real, vector_imaginary = vector[column]
        first, second = link_real * vector_real, link_real * vector_imaginary
        third, fourth = link_imaginary * vector_imaginary, link_imaginary * vector_real
        if adjoint:
            first, second = first + third, second - fourth
        else:
            first, second = first - third, second + fourth
        real = first if real is None else real + first
        imaginary = second if imaginary is None else imaginary + second
    return real, imaginary


def kernel(rs_hbm, links_hbm, clover_hbm, near_hbm, owners_hbm, smooth, sums,
           rs, links16, clover, near, owners, links, face_links, field, acc,
           outbox, inbox, tiles, placing, parcels, arrived,
           load_sem, send_sem, recv_sem, parcel_send, parcel_recv):
    groups = lax.axis_size("xy")
    slots = groups * MOST
    me = {axis: lax.axis_index(axis) for axis in ("ta", "gz", "xy")}

    def shifted(axis, offset):
        size = lax.axis_size(axis)
        return lax.rem(me[axis] + (offset + size), size)

    loads = [
        pltpu.make_async_copy(source, target, load_sem.at[i])
        for i, (source, target) in enumerate(
            ((links_hbm, links16), (rs_hbm, rs), (clover_hbm, clover), (near_hbm, near), (owners_hbm, owners))
        )
    ]
    for copy in loads[:3] + loads[4:]:
        copy.start()

    barrier = pltpu.get_barrier_semaphore()
    greeted = 0
    for axis in ("ta", "gz"):
        for offset in (1, -1):
            pl.semaphore_signal(barrier, inc=1, device_id={axis: shifted(axis, offset)}, device_id_type=MESH)
            greeted += 1
    for offset in range(1, groups):
        pl.semaphore_signal(barrier, inc=1, device_id={"xy": shifted("xy", offset)}, device_id_type=MESH)
        greeted += 1

    row8 = lax.broadcasted_iota(jnp.int32, (8, 128), 0)
    lane8 = lax.broadcasted_iota(jnp.int32, (8, 128), 1)
    upper_rows = row8 >= 4
    depth_at = row8 % 4
    width_at = lane8 // LY
    height_at = lane8 % LY

    def pack(values, mu, high):
        if mu == TIME:
            if high:
                return jnp.where(upper_rows, values[1][1], roll(values[0][1], 4, 0))
            return jnp.where(upper_rows, roll(values[1][0], 4, 0), values[0][0])
        axis, unit, at = (0, 1, depth_at) if mu == DEPTH else (1, LY, width_at)
        face = 3 if high else 0
        out = None
        for index in range(4):
            piece = roll(values[index // 2][index % 2], (index - face) * unit, axis)
            out = piece if out is None else jnp.where(at == index, piece, out)
        return out

    def unpack(packed, mu, high):
        if mu == TIME:
            if high:
                return [
                    (None, jnp.where(upper_rows, roll(packed, 4 * (1 - spin), 0), 0.0))
                    for spin in range(2)
                ]
            return [
                (jnp.where(upper_rows, 0.0, roll(packed, 4 * spin, 0)), None)
                for spin in range(2)
            ]
        axis, unit, at = (0, 1, depth_at) if mu == DEPTH else (1, LY, width_at)
        face = 3 if high else 0
        pieces = [
            jnp.where(at == face, roll(packed, (face - index) * unit, axis), 0.0)
            for index in range(4)
        ]
        return [(pieces[2 * spin], pieces[2 * spin + 1]) for spin in range(2)]

    def neighbour(value, mu, ahead):
        if mu == HEIGHT:
            step = -1 if ahead else 1
            edge = height_at == (LY - 1 if ahead else 0)
            return jnp.where(edge[None], roll(value, -step * (LY - 1), 2), roll(value, step, 2))
        if mu == TIME:
            turned = roll(value, 4, 1)
            if ahead:
                first = jnp.where(upper_rows, turned[1], turned[0])
                second = jnp.where(upper_rows, 0.0, turned[1])
            else:
                first = jnp.where(upper_rows, turned[0], 0.0)
                second = jnp.where(upper_rows, turned[1], turned[0])
            return jnp.stack([first, second])
        axis, unit, at = (1, 1, depth_at) if mu == DEPTH else (2, LY, width_at)
        edge = at == (3 if ahead else 0)
        return jnp.where(edge[None], 0.0, roll(value, -unit if ahead else unit, axis))

    def component(part, spin, color):
        return (part * 4 + spin) * 3 + color

    def load_field(spin, color):
        return field[component(0, spin, color)], field[component(1, spin, color)]

    def message(sweep, way, axis, offset):
        return pltpu.make_async_remote_copy(
            src_ref=outbox.at[sweep, way],
            dst_ref=inbox.at[sweep, way],
            send_sem=send_sem.at[sweep, way],
            recv_sem=recv_sem.at[sweep, way],
            device_id={axis: shifted(axis, offset)},
            device_id_type=MESH,
        )

    acc[...] = jnp.zeros(acc.shape, F32)
    smooth[...] = jnp.zeros(smooth.shape, F32)
    sums[...] = jnp.zeros(sums.shape, F32)

    loads[0].wait()
    for order, (mu, _) in enumerate(CROSSING):
        for part in range(2):
            for at in range(9):
                value = links16[mu, part, at].astype(F32).reshape(2, 8, 128)
                face_links[order, part, at] = pack([value, value], mu, True)
    loads[1].wait()
    loads[2].wait()

    def body(sweep, carry):
        kept = jnp.where(sweep == SWEEPS - 1, 1.0, 0.0)
        for chirality in range(2):
            vector = [
                [rs[component(part, 2 * chirality, j)] + HOPPING * acc[component(part, 2 * chirality, j)]
                 for part in range(2)]
                for j in range(6)
            ]
            for i in range(6):
                real = imaginary = None
                for j in range(6):
                    block_real = clover[chirality, 0, i * 6 + j].astype(F32).reshape(2, 8, 128)
                    block_imaginary = clover[chirality, 1, i * 6 + j].astype(F32).reshape(2, 8, 128)
                    first = block_real * vector[j][0] - block_imaginary * vector[j][1]
                    second = block_real * vector[j][1] + block_imaginary * vector[j][0]
                    real = first if real is None else real + first
                    imaginary = second if imaginary is None else imaginary + second
                for part, value in enumerate((real, imaginary)):
                    at = component(part, 2 * chirality, i)
                    field[at] = value - kept * smooth[at]
                    smooth[at] = value

        @pl.when(sweep == 0)
        def _():
            pl.semaphore_wait(barrier, greeted)

        for order, (mu, axis) in enumerate(CROSSING):
            half = project(load_field, mu, -1)
            for part in range(2):
                for color in range(3):
                    outbox[sweep, 2 * order, part * 3 + color] = pack(
                        [half[0][color][part], half[1][color][part]], mu, False)
        for order, (mu, axis) in enumerate(CROSSING):
            half = project(load_field, mu, 1)
            packed = [
                tuple(pack([half[0][color][part], half[1][color][part]], mu, True) for part in range(2))
                for color in range(3)
            ]

            def face_link(part, row, column, order=order):
                return face_links[order, part, row * 3 + column]

            for row in range(3):
                pair = color_row(face_link, packed, row, True)
                for part in range(2):
                    outbox[sweep, 2 * order + 1, part * 3 + row] = pair[part]
        for order, (mu, axis) in enumerate(CROSSING):
            message(sweep, 2 * order, axis, -1).start()
            message(sweep, 2 * order + 1, axis, 1).start()

        @pl.when(sweep == 0)
        def _():
            loads[3].start()
            loads[4].wait()
            owner = [owners[i] for i in range(AGGS)]
            target = []
            for i in range(AGGS):
                rank = jnp.int32(0)
                for j in range(i):
                    rank = rank + jnp.where(owner[j] == owner[i], 1, 0)
                target.append(owner[i] * MOST + rank)
            lane_from = lax.broadcasted_iota(jnp.int32, (128, 128), 0)
            lane_to = lax.broadcasted_iota(jnp.int32, (128, 128), 1)
            slot_of = jnp.zeros((128, 128), jnp.int32)
            for i in range(AGGS):
                slot_of = jnp.where((lane_from // 4) % AGGS == i, target[i], slot_of)
            same_site = (lane_from // LY) * 4 + lane_from % 4 == lane_to % 16
            for part in range(slots // 8):
                placing[:, part * 128:(part + 1) * 128] = jnp.where(
                    same_site & (slot_of == lane_to // 16 + part * 8), 1.0, 0.0
                ).astype(BF16)
            for mu in range(4):
                for part in range(2):
                    for at in range(9):
                        links[mu, part, at] = links16[mu, part, at].astype(F32).reshape(2, 8, 128)

        started = False
        for mu in (HEIGHT, TIME, DEPTH, WIDTH):
            def link(part, row, column, mu=mu):
                return links[mu, part, row * 3 + column]

            for sign in (-1, 1):
                half = project(load_field, mu, sign)
                if sign < 0:
                    half = [[tuple(neighbour(value, mu, True) for value in pair) for pair in spin] for spin in half]
                for row in range(3):
                    moved = []
                    for spin in range(2):
                        pair = color_row(link, half[spin], row, sign > 0)
                        if sign > 0:
                            pair = tuple(neighbour(value, mu, False) for value in pair)
                        moved.append(pair)
                    for spin in range(4):
                        places = [component(part, spin, row) for part in range(2)]
                        base = tuple(acc[at] for at in places) if started else (0.0, 0.0)
                        if spin < 2:
                            total = add_phase(base, moved[spin], 0, 1)
                        else:
                            source, power = LOWER[mu][spin - 2]
                            total = add_phase(base, moved[source], power, sign)
                        for at, value in zip(places, total):
                            acc[at] = value
                started = True

        for order, (mu, axis) in reversed(list(enumerate(CROSSING))):
            message(sweep, 2 * order, axis, -1).wait_recv()
            message(sweep, 2 * order + 1, axis, 1).wait_recv()

            def face_link(part, at_row, column, order=order):
                return face_links[order, part, at_row * 3 + column]

            for row in range(3):
                totals = [
                    [[acc[component(part, spin, row), side] for side in range(2)] for part in range(2)]
                    for spin in range(4)
                ]
                for sign in (-1, 1):
                    way = 2 * order + (0 if sign < 0 else 1)
                    if sign < 0:
                        packed = [
                            (inbox[sweep, way, color], inbox[sweep, way, 3 + color]) for color in range(3)
                        ]
                        pair = color_row(face_link, packed, row, False)
                    else:
                        pair = inbox[sweep, way, row], inbox[sweep, way, 3 + row]
                    spread = [unpack(value, mu, sign < 0) for value in pair]
                    for side in range(2):
                        if spread[0][0][side] is None:
                            continue
                        pieces = [(spread[0][spin][side], spread[1][spin][side]) for spin in range(2)]
                        for spin in range(4):
                            base = totals[spin][0][side], totals[spin][1][side]
                            if spin < 2:
                                total = add_phase(base, pieces[spin], 0, 1)
                            else:
                                source, power = LOWER[mu][spin - 2]
                                total = add_phase(base, pieces[source], power, sign)
                            totals[spin][0][side], totals[spin][1][side] = total
                for spin in range(4):
                    for part in range(2):
                        for side in range(2):
                            acc[component(part, spin, row), side] = totals[spin][part][side]
        return carry

    lax.fori_loop(0, SWEEPS, body, 0)

    for part in range(2):
        for color in range(3):
            for spin in range(4):
                value = HOPPING * acc[component(part, spin, color)]
                for side in range(2):
                    at = ((part * 3 + color) * 2 + side) * 4 + spin
                    tiles[at * 8:(at + 1) * 8, :] = value[side]
    rows = jnp.concatenate([tiles[pl.ds(r, 48, stride=8), :] for r in range(8)], axis=0).astype(BF16)
    mine = me["xy"]

    def parcel(owner):
        return pltpu.make_async_remote_copy(
            src_ref=parcels.at[owner],
            dst_ref=arrived.at[mine],
            send_sem=parcel_send.at[owner],
            recv_sem=parcel_recv.at[mine],
            device_id={"xy": owner},
            device_id_type=MESH,
        )

    lane = lax.broadcasted_iota(jnp.int32, (48, 128), 1) // 16
    flags = {step: jnp.where((lane & step) != 0, 1.0, 0.0).astype(BF16) for step in (1, 2, 4)}
    for part in range(slots // 8):
        placed = jnp.dot(rows, placing[:, part * 128:(part + 1) * 128], preferred_element_type=F32)
        parts = [placed[r * 48:(r + 1) * 48, :].astype(BF16) for r in range(8)]
        for step in (4, 2, 1):
            for r in range(8):
                if r & step:
                    continue
                first, second = parts[r], parts[r + step]
                odd = flags[step] > 0
                parts[r] = jnp.where(odd, roll(second, step * 16, 1), first)
                parts[r + step] = jnp.where(odd, second, roll(first, -step * 16, 1))
        for r in range(8):
            slot = part * 8 + r
            parcels[slot // MOST, slot % MOST] = parts[r]
    for turn in sorted(range(1, groups), key=lambda o: -min(o, groups - o)):
        parcel(lax.rem(mine + turn, groups)).start()

    loads[3].wait()

    def contract(index, carry):
        pair = index // 2
        away = jnp.where(pair == 2, groups // 2 - 1, jnp.where(pair == 3, groups // 2 - 2, pair))
        chip = lax.rem(mine // 2 + away, groups // 2)
        source = chip * 2 + lax.rem(mine + index, 2)

        @pl.when(index > 0)
        def _():
            pltpu.make_async_remote_copy(
                src_ref=parcels.at[source],
                dst_ref=arrived.at[source],
                send_sem=parcel_send.at[source],
                recv_sem=parcel_recv.at[source],
                device_id={"xy": source},
                device_id_type=MESH,
            ).wait_recv()

        @pl.when(index == 0)
        def _():
            arrived[mine] = parcels[mine]

        for m in range(MOST):
            slot = source * MOST + m
            tile = arrived[source, m].astype(F32).reshape(6, 8, 128)
            turned = jnp.concatenate([tile[3:], -tile[:3]], axis=0)
            for v in range(NV):
                vector = near[slot * NV + v].astype(F32).reshape(6, 8, 128)
                for part, other in enumerate((tile, turned)):
                    total = jnp.sum(jnp.sum(vector * other, axis=0), axis=1, keepdims=True)
                    sums[v * 2 + part] = jnp.where(lane8 == slot, total, sums[v * 2 + part])
        return carry

    lax.fori_loop(0, groups, contract, 0)
    for sweep in range(SWEEPS):
        for order, (mu, axis) in enumerate(CROSSING):
            message(sweep, 2 * order, axis, -1).wait_send()
            message(sweep, 2 * order + 1, axis, 1).wait_send()
    for turn in range(1, groups):
        parcel(lax.rem(mine + turn, groups)).wait_send()


def finish(smooth, sums, smoothed, coarse, staged, sems):
    first = pltpu.make_async_copy(smooth, smoothed, sems.at[0])
    first.start()
    slots = coarse.shape[-1]
    total = sums[...]
    total = total + roll(total, 4, 1)
    total = total + roll(total, -1, 1)
    total = total.reshape(NV, 2, 8, 128)
    for chirality in range(2):
        staged[chirality] = total[:, :, 2 * chirality, :slots]
    second = pltpu.make_async_copy(staged, coarse, sems.at[1])
    second.start()
    first.wait()
    second.wait()


def shards(right_side, links, clover_inverse, near_null, owners):
    groups = lax.axis_size("xy")
    slots = groups * MOST
    near = jnp.transpose(near_null[0, 0, 0], (0, 1, 2, 4, 3, 5)).reshape(slots, NV, 2, 3, 4, 2, 128)
    near = jnp.transpose(near, (0, 1, 2, 3, 5, 4, 6)).reshape(slots * NV, 48, 128)
    anywhere = pl.BlockSpec(memory_space=pl.ANY)
    vmem = pltpu.VMEM
    inside = pl.BlockSpec(memory_space=vmem)
    operands = [
        pltpu.with_memory_space_constraint(value, pltpu.HBM)
        for value in (
            right_side.reshape(24, 2, 8, 128),
            links.reshape(4, 2, 9, 16, 128),
            clover_inverse.reshape(2, 2, 36, 16, 128),
            near,
            owners.reshape(-1),
        )
    ]
    smooth, sums = pl.pallas_call(
        kernel,
        out_shape=(vmem((24, 2, 8, 128), F32), vmem((NV * 2, 8, 128), F32)),
        in_specs=[anywhere] * 5,
        out_specs=(inside, inside),
        scratch_shapes=[
            vmem((24, 2, 8, 128), F32),
            vmem((4, 2, 9, 16, 128), BF16),
            vmem((2, 2, 36, 16, 128), BF16),
            vmem((slots * NV, 48, 128), BF16),
            pltpu.SMEM((AGGS,), jnp.int32),
            vmem((4, 2, 9, 2, 8, 128), F32),
            vmem((3, 2, 9, 8, 128), F32),
            vmem((24, 2, 8, 128), F32),
            vmem((24, 2, 8, 128), F32),
            vmem((SWEEPS, 6, 6, 8, 128), F32),
            vmem((SWEEPS, 6, 6, 8, 128), F32),
            vmem((384, 128), F32),
            vmem((128, slots * 16), BF16),
            vmem((groups, MOST, 48, 128), BF16),
            vmem((groups, MOST, 48, 128), BF16),
            pltpu.SemaphoreType.DMA((5,)),
            pltpu.SemaphoreType.DMA((SWEEPS, 6)),
            pltpu.SemaphoreType.DMA((SWEEPS, 6)),
            pltpu.SemaphoreType.DMA((groups,)),
            pltpu.SemaphoreType.DMA((groups,)),
        ],
        compiler_params=pltpu.CompilerParams(
            collective_id=0, has_side_effects=True, vmem_limit_bytes=32 * 1024 * 1024
        ),
        name="smooth_and_restrict",
    )(*operands)
    smoothed, coarse = pl.pallas_call(
        finish,
        out_shape=(
            jax.ShapeDtypeStruct((24, 2, 8, 128), F32),
            jax.ShapeDtypeStruct((2, NV, 2, slots), F32),
        ),
        in_specs=[anywhere, inside],
        out_specs=(anywhere, anywhere),
        scratch_shapes=[vmem((2, NV, 2, slots), F32), pltpu.SemaphoreType.DMA((2,))],
        compiler_params=pltpu.CompilerParams(vmem_limit_bytes=32 * 1024 * 1024),
        name="finish",
    )(smooth, sums)
    coarse = jnp.transpose(coarse, (3, 0, 2, 1))[None, None, None]
    return smoothed.reshape(2, 4, 3, 4, 4, 128), coarse


def solution(mesh):
    placed = (
        P(None, None, None, "ta", "gz", "xy"),
        P(None, None, None, None, "ta", "gz", "xy"),
        P(None, None, None, None, "ta", "gz", "xy"),
        P("ta", "gz", "xy", None, None, None, None, None, None),
        P("ta", "gz", "xy", None),
    )
    return jax.shard_map(
        shards,
        mesh=mesh,
        in_specs=placed,
        out_specs=(
            P(None, None, None, "ta", "gz", "xy"),
            P("ta", "gz", "xy", None, None, None, None),
        ),
        check_vma=False,
    )
```

```python
import jax
import jax.numpy as jnp
from jax import lax
from jax.experimental import pallas as pl
from jax.experimental.pallas import tpu as pltpu
from jax.sharding import PartitionSpec as P

LY = 32
SWEEPS = 3
MOST = 2
AGGS = 8
NV = 12
HOPPING = 0.13
F32 = jnp.float32
BF16 = jnp.bfloat16
MESH = pl.DeviceIdType.MESH
WIDTH, HEIGHT, DEPTH, TIME = range(4)
CROSSING = ((TIME, "ta"), (DEPTH, "gz"), (WIDTH, "xy"))
UPPER = {
    WIDTH: ((1, 3), (0, 3)),
    HEIGHT: ((1, 2), (0, 0)),
    DEPTH: ((0, 3), (1, 1)),
    TIME: ((0, 0), (1, 0)),
}
LOWER = {
    WIDTH: ((1, 1), (0, 1)),
    HEIGHT: ((1, 0), (0, 2)),
    DEPTH: ((0, 1), (1, 3)),
    TIME: ((0, 0), (1, 0)),
}


def roll(value, shift, axis):
    size = value.shape[axis]
    shift = shift % size
    return value if shift == 0 else pltpu.roll(value, shift, axis)


def add_phase(base, pair, power, sign):
    if sign < 0:
        power = power + 2
    real, imaginary = pair
    turned = ((real, 1), (imaginary, 1)), ((imaginary, -1), (real, 1)), ((real, -1), (imaginary, -1)), ((imaginary, 1), (real, -1))
    out = []
    for part, (value, factor) in zip(base, turned[power % 4]):
        out.append(part + value if factor > 0 else part - value)
    return tuple(out)


def project(load, mu, sign):
    half = []
    for spin in range(2):
        source, power = UPPER[mu][spin]
        half.append([
            add_phase(load(spin, color), load(2 + source, color), power, sign)
            for color in range(3)
        ])
    return half


def color_row(link, vector, row, adjoint):
    real = imaginary = None
    for column in range(3):
        at = (column, row) if adjoint else (row, column)
        link_real, link_imaginary = link(0, *at), link(1, *at)
        vector_real, vector_imaginary = vector[column]
        first, second = link_real * vector_real, link_real * vector_imaginary
        third, fourth = link_imaginary * vector_imaginary, link_imaginary * vector_real
        if adjoint:
            first, second = first + third, second - fourth
        else:
            first, second = first - third, second + fourth
        real = first if real is None else real + first
        imaginary = second if imaginary is None else imaginary + second
    return real, imaginary


def kernel(rs_hbm, links_hbm, clover_hbm, near_hbm, owners_hbm, smooth, sums,
           rs, links16, clover, near, owners, links, face_links, field, acc,
           outbox, inbox, tiles, placing, parcels, arrived,
           load_sem, send_sem, recv_sem, parcel_send, parcel_recv):
    groups = lax.axis_size("xy")
    slots = groups * MOST
    me = {axis: lax.axis_index(axis) for axis in ("ta", "gz", "xy")}

    def shifted(axis, offset):
        size = lax.axis_size(axis)
        return lax.rem(me[axis] + (offset + size), size)

    loads = [
        pltpu.make_async_copy(source, target, load_sem.at[i])
        for i, (source, target) in enumerate(
            ((links_hbm, links16), (rs_hbm, rs), (clover_hbm, clover), (near_hbm, near), (owners_hbm, owners))
        )
    ]
    for copy in loads[:3] + loads[4:]:
        copy.start()

    barrier = pltpu.get_barrier_semaphore()
    greeted = 0
    for axis in ("ta", "gz"):
        for offset in (1, -1):
            pl.semaphore_signal(barrier, inc=1, device_id={axis: shifted(axis, offset)}, device_id_type=MESH)
            greeted += 1
    for offset in range(1, groups):
        pl.semaphore_signal(barrier, inc=1, device_id={"xy": shifted("xy", offset)}, device_id_type=MESH)
        greeted += 1

    row8 = lax.broadcasted_iota(jnp.int32, (8, 128), 0)
    lane8 = lax.broadcasted_iota(jnp.int32, (8, 128), 1)
    upper_rows = row8 >= 4
    depth_at = row8 % 4
    width_at = lane8 // LY
    height_at = lane8 % LY

    def pack(values, mu, high):
        if mu == TIME:
            if high:
                return jnp.where(upper_rows, values[1][1], roll(values[0][1], 4, 0))
            return jnp.where(upper_rows, roll(values[1][0], 4, 0), values[0][0])
        axis, unit, at = (0, 1, depth_at) if mu == DEPTH else (1, LY, width_at)
        face = 3 if high else 0
        out = None
        for index in range(4):
            piece = roll(values[index // 2][index % 2], (index - face) * unit, axis)
            out = piece if out is None else jnp.where(at == index, piece, out)
        return out

    def unpack(packed, mu, high):
        if mu == TIME:
            if high:
                return [
                    (None, jnp.where(upper_rows, roll(packed, 4 * (1 - spin), 0), 0.0))
                    for spin in range(2)
                ]
            return [
                (jnp.where(upper_rows, 0.0, roll(packed, 4 * spin, 0)), None)
                for spin in range(2)
            ]
        axis, unit, at = (0, 1, depth_at) if mu == DEPTH else (1, LY, width_at)
        face = 3 if high else 0
        pieces = [
            jnp.where(at == face, roll(packed, (face - index) * unit, axis), 0.0)
            for index in range(4)
        ]
        return [(pieces[2 * spin], pieces[2 * spin + 1]) for spin in range(2)]

    def neighbour(value, mu, ahead):
        if mu == HEIGHT:
            step = -1 if ahead else 1
            edge = height_at == (LY - 1 if ahead else 0)
            return jnp.where(edge[None], roll(value, -step * (LY - 1), 2), roll(value, step, 2))
        if mu == TIME:
            turned = roll(value, 4, 1)
            if ahead:
                first = jnp.where(upper_rows, turned[1], turned[0])
                second = jnp.where(upper_rows, 0.0, turned[1])
            else:
                first = jnp.where(upper_rows, turned[0], 0.0)
                second = jnp.where(upper_rows, turned[1], turned[0])
            return jnp.stack([first, second])
        axis, unit, at = (1, 1, depth_at) if mu == DEPTH else (2, LY, width_at)
        edge = at == (3 if ahead else 0)
        return jnp.where(edge[None], 0.0, roll(value, -unit if ahead else unit, axis))

    def component(part, spin, color):
        return (part * 4 + spin) * 3 + color

    def load_field(spin, color):
        return field[component(0, spin, color)], field[component(1, spin, color)]

    def message(sweep, way, axis, offset):
        return pltpu.make_async_remote_copy(
            src_ref=outbox.at[sweep, way],
            dst_ref=inbox.at[sweep, way],
            send_sem=send_sem.at[sweep, way],
            recv_sem=recv_sem.at[sweep, way],
            device_id={axis: shifted(axis, offset)},
            device_id_type=MESH,
        )

    acc[...] = jnp.zeros(acc.shape, F32)
    smooth[...] = jnp.zeros(smooth.shape, F32)
    sums[...] = jnp.zeros(sums.shape, F32)

    loads[0].wait()
    for order, (mu, _) in enumerate(CROSSING):
        for part in range(2):
            for at in range(9):
                value = links16[mu, part, at].astype(F32).reshape(2, 8, 128)
                face_links[order, part, at] = pack([value, value], mu, True)
    loads[1].wait()
    loads[2].wait()

    def body(sweep, carry):
        kept = jnp.where(sweep == SWEEPS - 1, 1.0, 0.0)
        for chirality in range(2):
            vector = [
                [rs[component(part, 2 * chirality, j)] + HOPPING * acc[component(part, 2 * chirality, j)]
                 for part in range(2)]
                for j in range(6)
            ]
            for i in range(6):
                real = imaginary = None
                for j in range(6):
                    block_real = clover[chirality, 0, i * 6 + j].astype(F32).reshape(2, 8, 128)
                    block_imaginary = clover[chirality, 1, i * 6 + j].astype(F32).reshape(2, 8, 128)
                    first = block_real * vector[j][0] - block_imaginary * vector[j][1]
                    second = block_real * vector[j][1] + block_imaginary * vector[j][0]
                    real = first if real is None else real + first
                    imaginary = second if imaginary is None else imaginary + second
                for part, value in enumerate((real, imaginary)):
                    at = component(part, 2 * chirality, i)
                    field[at] = value - kept * smooth[at]
                    smooth[at] = value

        @pl.when(sweep == 0)
        def _():
            pl.semaphore_wait(barrier, greeted)

        for order, (mu, axis) in enumerate(CROSSING):
            half = project(load_field, mu, -1)
            for part in range(2):
                for color in range(3):
                    outbox[sweep, 2 * order, part * 3 + color] = pack(
                        [half[0][color][part], half[1][color][part]], mu, False)
        for order, (mu, axis) in enumerate(CROSSING):
            half = project(load_field, mu, 1)
            packed = [
                tuple(pack([half[0][color][part], half[1][color][part]], mu, True) for part in range(2))
                for color in range(3)
            ]

            def face_link(part, row, column, order=order):
                return face_links[order, part, row * 3 + column]

            for row in range(3):
                pair = color_row(face_link, packed, row, True)
                for part in range(2):
                    outbox[sweep, 2 * order + 1, part * 3 + row] = pair[part]
        for order, (mu, axis) in enumerate(CROSSING):
            message(sweep, 2 * order, axis, -1).start()
            message(sweep, 2 * order + 1, axis, 1).start()

        @pl.when(sweep == 0)
        def _():
            loads[3].start()
            loads[4].wait()
            owner = [owners[i] for i in range(AGGS)]
            target = []
            for i in range(AGGS):
                rank = jnp.int32(0)
                for j in range(i):
                    rank = rank + jnp.where(owner[j] == owner[i], 1, 0)
                target.append(owner[i] * MOST + rank)
            lane_from = lax.broadcasted_iota(jnp.int32, (128, 128), 0)
            lane_to = lax.broadcasted_iota(jnp.int32, (128, 128), 1)
            slot_of = jnp.zeros((128, 128), jnp.int32)
            for i in range(AGGS):
                slot_of = jnp.where((lane_from // 4) % AGGS == i, target[i], slot_of)
            same_site = (lane_from // LY) * 4 + lane_from % 4 == lane_to % 16
            for part in range(slots // 8):
                placing[:, part * 128:(part + 1) * 128] = jnp.where(
                    same_site & (slot_of == lane_to // 16 + part * 8), 1.0, 0.0
                ).astype(BF16)
            for mu in range(4):
                for part in range(2):
                    for at in range(9):
                        links[mu, part, at] = links16[mu, part, at].astype(F32).reshape(2, 8, 128)

        started = False
        for mu in (HEIGHT, TIME, DEPTH, WIDTH):
            def link(part, row, column, mu=mu):
                return links[mu, part, row * 3 + column]

            for sign in (-1, 1):
                half = project(load_field, mu, sign)
                if sign < 0:
                    half = [[tuple(neighbour(value, mu, True) for value in pair) for pair in spin] for spin in half]
                for row in range(3):
                    moved = []
                    for spin in range(2):
                        pair = color_row(link, half[spin], row, sign > 0)
                        if sign > 0:
                            pair = tuple(neighbour(value, mu, False) for value in pair)
                        moved.append(pair)
                    for spin in range(4):
                        places = [component(part, spin, row) for part in range(2)]
                        base = tuple(acc[at] for at in places) if started else (0.0, 0.0)
                        if spin < 2:
                            total = add_phase(base, moved[spin], 0, 1)
                        else:
                            source, power = LOWER[mu][spin - 2]
                            total = add_phase(base, moved[source], power, sign)
                        for at, value in zip(places, total):
                            acc[at] = value
                started = True

        for order, (mu, axis) in reversed(list(enumerate(CROSSING))):
            message(sweep, 2 * order, axis, -1).wait_recv()
            message(sweep, 2 * order + 1, axis, 1).wait_recv()

            def face_link(part, at_row, column, order=order):
                return face_links[order, part, at_row * 3 + column]

            for row in range(3):
                totals = [
                    [[acc[component(part, spin, row), side] for side in range(2)] for part in range(2)]
                    for spin in range(4)
                ]
                for sign in (-1, 1):
                    way = 2 * order + (0 if sign < 0 else 1)
                    if sign < 0:
                        packed = [
                            (inbox[sweep, way, color], inbox[sweep, way, 3 + color]) for color in range(3)
                        ]
                        pair = color_row(face_link, packed, row, False)
                    else:
                        pair = inbox[sweep, way, row], inbox[sweep, way, 3 + row]
                    spread = [unpack(value, mu, sign < 0) for value in pair]
                    for side in range(2):
                        if spread[0][0][side] is None:
                            continue
                        pieces = [(spread[0][spin][side], spread[1][spin][side]) for spin in range(2)]
                        for spin in range(4):
                            base = totals[spin][0][side], totals[spin][1][side]
                            if spin < 2:
                                total = add_phase(base, pieces[spin], 0, 1)
                            else:
                                source, power = LOWER[mu][spin - 2]
                                total = add_phase(base, pieces[source], power, sign)
                            totals[spin][0][side], totals[spin][1][side] = total
                for spin in range(4):
                    for part in range(2):
                        for side in range(2):
                            acc[component(part, spin, row), side] = totals[spin][part][side]
        return carry

    lax.fori_loop(0, SWEEPS, body, 0)

    for part in range(2):
        for color in range(3):
            for spin in range(4):
                value = HOPPING * acc[component(part, spin, color)]
                for side in range(2):
                    at = ((part * 3 + color) * 2 + side) * 4 + spin
                    tiles[at * 8:(at + 1) * 8, :] = value[side]
    rows = jnp.concatenate([tiles[pl.ds(r, 48, stride=8), :] for r in range(8)], axis=0).astype(BF16)
    mine = me["xy"]

    def parcel(owner):
        return pltpu.make_async_remote_copy(
            src_ref=parcels.at[owner],
            dst_ref=arrived.at[mine],
            send_sem=parcel_send.at[owner],
            recv_sem=parcel_recv.at[mine],
            device_id={"xy": owner},
            device_id_type=MESH,
        )

    placed = jnp.dot(rows, placing[...], preferred_element_type=F32)
    lane = lax.broadcasted_iota(jnp.int32, (48, 128), 1) // 16
    flags = {step: jnp.where((lane & step) != 0, 1.0, 0.0).astype(BF16) for step in (1, 2, 4)}
    for part in range(slots // 8):
        parts = [placed[r * 48:(r + 1) * 48, part * 128:(part + 1) * 128].astype(BF16) for r in range(8)]
        for step in (4, 2, 1):
            for r in range(8):
                if r & step:
                    continue
                first, second = parts[r], parts[r + step]
                odd = flags[step] > 0
                parts[r] = jnp.where(odd, roll(second, step * 16, 1), first)
                parts[r + step] = jnp.where(odd, second, roll(first, -step * 16, 1))
        for r in range(8):
            slot = part * 8 + r
            parcels[slot // MOST, slot % MOST] = parts[r]
    for turn in sorted(range(1, groups), key=lambda o: -min(o, groups - o)):
        parcel(lax.rem(mine + turn, groups)).start()

    for sweep in range(SWEEPS):
        for order, (mu, axis) in enumerate(CROSSING):
            message(sweep, 2 * order, axis, -1).wait_send()
            message(sweep, 2 * order + 1, axis, 1).wait_send()
    loads[3].wait()

    def contract(index, carry):
        pair = index // 2
        away = jnp.where(pair == 2, groups // 2 - 1, jnp.where(pair == 3, groups // 2 - 2, pair))
        chip = lax.rem(mine // 2 + away, groups // 2)
        source = chip * 2 + lax.rem(mine + index, 2)

        @pl.when(index > 0)
        def _():
            pltpu.make_async_remote_copy(
                src_ref=parcels.at[source],
                dst_ref=arrived.at[source],
                send_sem=parcel_send.at[source],
                recv_sem=parcel_recv.at[source],
                device_id={"xy": source},
                device_id_type=MESH,
            ).wait_recv()

        @pl.when(index == 0)
        def _():
            arrived[mine] = parcels[mine]

        for m in range(MOST):
            slot = source * MOST + m
            tile = arrived[source, m].astype(F32).reshape(6, 8, 128)
            turned = jnp.concatenate([tile[3:], -tile[:3]], axis=0)
            for v in range(NV):
                vector = near[slot * NV + v].astype(F32).reshape(6, 8, 128)
                for part, other in enumerate((tile, turned)):
                    total = jnp.sum(jnp.sum(vector * other, axis=0), axis=1, keepdims=True)
                    sums[v * 2 + part] = jnp.where(lane8 == slot, total, sums[v * 2 + part])
        return carry

    lax.fori_loop(0, groups, contract, 0)
    for turn in range(1, groups):
        parcel(lax.rem(mine + turn, groups)).wait_send()


def finish(smooth, sums, smoothed, coarse, staged, sems):
    first = pltpu.make_async_copy(smooth, smoothed, sems.at[0])
    first.start()
    slots = coarse.shape[-1]
    total = sums[...]
    total = total + roll(total, 4, 1)
    total = total + roll(total, -1, 1)
    total = total.reshape(NV, 2, 8, 128)
    for chirality in range(2):
        staged[chirality] = total[:, :, 2 * chirality, :slots]
    second = pltpu.make_async_copy(staged, coarse, sems.at[1])
    second.start()
    first.wait()
    second.wait()


def shards(right_side, links, clover_inverse, near_null, owners):
    groups = lax.axis_size("xy")
    slots = groups * MOST
    near = jnp.transpose(near_null[0, 0, 0], (0, 1, 2, 4, 3, 5)).reshape(slots, NV, 2, 3, 4, 2, 128)
    near = jnp.transpose(near, (0, 1, 2, 3, 5, 4, 6)).reshape(slots * NV, 48, 128)
    anywhere = pl.BlockSpec(memory_space=pl.ANY)
    vmem = pltpu.VMEM
    inside = pl.BlockSpec(memory_space=vmem)
    operands = [
        pltpu.with_memory_space_constraint(value, pltpu.HBM)
        for value in (
            right_side.reshape(24, 2, 8, 128),
            links.reshape(4, 2, 9, 16, 128),
            clover_inverse.reshape(2, 2, 36, 16, 128),
            near,
            owners.reshape(-1),
        )
    ]
    smooth, sums = pl.pallas_call(
        kernel,
        out_shape=(vmem((24, 2, 8, 128), F32), vmem((NV * 2, 8, 128), F32)),
        in_specs=[anywhere] * 5,
        out_specs=(inside, inside),
        scratch_shapes=[
            vmem((24, 2, 8, 128), F32),
            vmem((4, 2, 9, 16, 128), BF16),
            vmem((2, 2, 36, 16, 128), BF16),
            vmem((slots * NV, 48, 128), BF16),
            pltpu.SMEM((AGGS,), jnp.int32),
            vmem((4, 2, 9, 2, 8, 128), F32),
            vmem((3, 2, 9, 8, 128), F32),
            vmem((24, 2, 8, 128), F32),
            vmem((24, 2, 8, 128), F32),
            vmem((SWEEPS, 6, 6, 8, 128), F32),
            vmem((SWEEPS, 6, 6, 8, 128), F32),
            vmem((384, 128), F32),
            vmem((128, slots * 16), BF16),
            vmem((groups, MOST, 48, 128), BF16),
            vmem((groups, MOST, 48, 128), BF16),
            pltpu.SemaphoreType.DMA((5,)),
            pltpu.SemaphoreType.DMA((SWEEPS, 6)),
            pltpu.SemaphoreType.DMA((SWEEPS, 6)),
            pltpu.SemaphoreType.DMA((groups,)),
            pltpu.SemaphoreType.DMA((groups,)),
        ],
        compiler_params=pltpu.CompilerParams(
            collective_id=0, has_side_effects=True, vmem_limit_bytes=32 * 1024 * 1024
        ),
        name="smooth_and_restrict",
    )(*operands)
    smoothed, coarse = pl.pallas_call(
        finish,
        out_shape=(
            jax.ShapeDtypeStruct((24, 2, 8, 128), F32),
            jax.ShapeDtypeStruct((2, NV, 2, slots), F32),
        ),
        in_specs=[anywhere, inside],
        out_specs=(anywhere, anywhere),
        scratch_shapes=[vmem((2, NV, 2, slots), F32), pltpu.SemaphoreType.DMA((2,))],
        compiler_params=pltpu.CompilerParams(vmem_limit_bytes=32 * 1024 * 1024),
        name="finish",
    )(smooth, sums)
    coarse = jnp.transpose(coarse, (3, 0, 2, 1))[None, None, None]
    return smoothed.reshape(2, 4, 3, 4, 4, 128), coarse


def solution(mesh):
    placed = (
        P(None, None, None, "ta", "gz", "xy"),
        P(None, None, None, None, "ta", "gz", "xy"),
        P(None, None, None, None, "ta", "gz", "xy"),
        P("ta", "gz", "xy", None, None, None, None, None, None),
        P("ta", "gz", "xy", None),
    )
    return jax.shard_map(
        shards,
        mesh=mesh,
        in_specs=placed,
        out_specs=(
            P(None, None, None, "ta", "gz", "xy"),
            P("ta", "gz", "xy", None, None, None, None),
        ),
        check_vma=False,
    )
```

```python
import jax
import jax.numpy as jnp
from jax import lax
from jax.experimental import pallas as pl
from jax.experimental.pallas import tpu as pltpu
from jax.sharding import PartitionSpec as P

LY = 32
SWEEPS = 3
MOST = 2
AGGS = 8
NV = 12
HOPPING = 0.13
F32 = jnp.float32
BF16 = jnp.bfloat16
MESH = pl.DeviceIdType.MESH
WIDTH, HEIGHT, DEPTH, TIME = range(4)
CROSSING = ((TIME, "ta"), (DEPTH, "gz"), (WIDTH, "xy"))
UPPER = {
    WIDTH: ((1, 3), (0, 3)),
    HEIGHT: ((1, 2), (0, 0)),
    DEPTH: ((0, 3), (1, 1)),
    TIME: ((0, 0), (1, 0)),
}
LOWER = {
    WIDTH: ((1, 1), (0, 1)),
    HEIGHT: ((1, 0), (0, 2)),
    DEPTH: ((0, 1), (1, 3)),
    TIME: ((0, 0), (1, 0)),
}


def roll(value, shift, axis):
    size = value.shape[axis]
    shift = shift % size
    return value if shift == 0 else pltpu.roll(value, shift, axis)


def add_phase(base, pair, power, sign):
    if sign < 0:
        power = power + 2
    real, imaginary = pair
    turned = ((real, 1), (imaginary, 1)), ((imaginary, -1), (real, 1)), ((real, -1), (imaginary, -1)), ((imaginary, 1), (real, -1))
    out = []
    for part, (value, factor) in zip(base, turned[power % 4]):
        out.append(part + value if factor > 0 else part - value)
    return tuple(out)


def project(load, mu, sign):
    half = []
    for spin in range(2):
        source, power = UPPER[mu][spin]
        half.append([
            add_phase(load(spin, color), load(2 + source, color), power, sign)
            for color in range(3)
        ])
    return half


def color_row(link, vector, row, adjoint):
    real = imaginary = None
    for column in range(3):
        at = (column, row) if adjoint else (row, column)
        link_real, link_imaginary = link(0, *at), link(1, *at)
        vector_real, vector_imaginary = vector[column]
        first, second = link_real * vector_real, link_real * vector_imaginary
        third, fourth = link_imaginary * vector_imaginary, link_imaginary * vector_real
        if adjoint:
            first, second = first + third, second - fourth
        else:
            first, second = first - third, second + fourth
        real = first if real is None else real + first
        imaginary = second if imaginary is None else imaginary + second
    return real, imaginary


def kernel(rs_hbm, links_hbm, clover_hbm, near_hbm, owners_hbm, smooth, sums,
           rs, links16, clover, near, near32, owners, links, face_links, field, acc,
           outbox, inbox, tiles, placing, parcels, arrived,
           load_sem, send_sem, recv_sem, parcel_send, parcel_recv):
    groups = lax.axis_size("xy")
    slots = groups * MOST
    me = {axis: lax.axis_index(axis) for axis in ("ta", "gz", "xy")}

    def shifted(axis, offset):
        size = lax.axis_size(axis)
        return lax.rem(me[axis] + (offset + size), size)

    loads = [
        pltpu.make_async_copy(source, target, load_sem.at[i])
        for i, (source, target) in enumerate(
            ((links_hbm, links16), (rs_hbm, rs), (clover_hbm, clover), (near_hbm, near), (owners_hbm, owners))
        )
    ]
    for copy in loads[:3] + loads[4:]:
        copy.start()

    barrier = pltpu.get_barrier_semaphore()
    greeted = 0
    for axis in ("ta", "gz"):
        for offset in (1, -1):
            pl.semaphore_signal(barrier, inc=1, device_id={axis: shifted(axis, offset)}, device_id_type=MESH)
            greeted += 1
    for offset in range(1, groups):
        pl.semaphore_signal(barrier, inc=1, device_id={"xy": shifted("xy", offset)}, device_id_type=MESH)
        greeted += 1

    row8 = lax.broadcasted_iota(jnp.int32, (8, 128), 0)
    lane8 = lax.broadcasted_iota(jnp.int32, (8, 128), 1)
    upper_rows = row8 >= 4
    depth_at = row8 % 4
    width_at = lane8 // LY
    height_at = lane8 % LY

    def pack(values, mu, high):
        if mu == TIME:
            if high:
                return jnp.where(upper_rows, values[1][1], roll(values[0][1], 4, 0))
            return jnp.where(upper_rows, roll(values[1][0], 4, 0), values[0][0])
        axis, unit, at = (0, 1, depth_at) if mu == DEPTH else (1, LY, width_at)
        face = 3 if high else 0
        out = None
        for index in range(4):
            piece = roll(values[index // 2][index % 2], (index - face) * unit, axis)
            out = piece if out is None else jnp.where(at == index, piece, out)
        return out

    def unpack(packed, mu, high):
        if mu == TIME:
            if high:
                return [
                    (None, jnp.where(upper_rows, roll(packed, 4 * (1 - spin), 0), 0.0))
                    for spin in range(2)
                ]
            return [
                (jnp.where(upper_rows, 0.0, roll(packed, 4 * spin, 0)), None)
                for spin in range(2)
            ]
        axis, unit, at = (0, 1, depth_at) if mu == DEPTH else (1, LY, width_at)
        face = 3 if high else 0
        pieces = [
            jnp.where(at == face, roll(packed, (face - index) * unit, axis), 0.0)
            for index in range(4)
        ]
        return [(pieces[2 * spin], pieces[2 * spin + 1]) for spin in range(2)]

    def neighbour(value, mu, ahead):
        if mu == HEIGHT:
            step = -1 if ahead else 1
            edge = height_at == (LY - 1 if ahead else 0)
            return jnp.where(edge[None], roll(value, -step * (LY - 1), 2), roll(value, step, 2))
        if mu == TIME:
            turned = roll(value, 4, 1)
            if ahead:
                first = jnp.where(upper_rows, turned[1], turned[0])
                second = jnp.where(upper_rows, 0.0, turned[1])
            else:
                first = jnp.where(upper_rows, turned[0], 0.0)
                second = jnp.where(upper_rows, turned[1], turned[0])
            return jnp.stack([first, second])
        axis, unit, at = (1, 1, depth_at) if mu == DEPTH else (2, LY, width_at)
        edge = at == (3 if ahead else 0)
        return jnp.where(edge[None], 0.0, roll(value, -unit if ahead else unit, axis))

    def component(part, spin, color):
        return (part * 4 + spin) * 3 + color

    def load_field(spin, color):
        return field[component(0, spin, color)], field[component(1, spin, color)]

    def message(sweep, way, axis, offset):
        return pltpu.make_async_remote_copy(
            src_ref=outbox.at[sweep, way],
            dst_ref=inbox.at[sweep, way],
            send_sem=send_sem.at[sweep, way],
            recv_sem=recv_sem.at[sweep, way],
            device_id={axis: shifted(axis, offset)},
            device_id_type=MESH,
        )

    acc[...] = jnp.zeros(acc.shape, F32)
    smooth[...] = jnp.zeros(smooth.shape, F32)
    sums[...] = jnp.zeros(sums.shape, F32)

    loads[0].wait()
    for order, (mu, _) in enumerate(CROSSING):
        for part in range(2):
            for at in range(9):
                value = links16[mu, part, at].astype(F32).reshape(2, 8, 128)
                face_links[order, part, at] = pack([value, value], mu, True)
    loads[1].wait()
    loads[2].wait()

    def body(sweep, carry):
        kept = jnp.where(sweep == SWEEPS - 1, 1.0, 0.0)
        for chirality in range(2):
            vector = [
                [rs[component(part, 2 * chirality, j)] + HOPPING * acc[component(part, 2 * chirality, j)]
                 for part in range(2)]
                for j in range(6)
            ]
            for i in range(6):
                real = imaginary = None
                for j in range(6):
                    block_real = clover[chirality, 0, i * 6 + j].astype(F32).reshape(2, 8, 128)
                    block_imaginary = clover[chirality, 1, i * 6 + j].astype(F32).reshape(2, 8, 128)
                    first = block_real * vector[j][0] - block_imaginary * vector[j][1]
                    second = block_real * vector[j][1] + block_imaginary * vector[j][0]
                    real = first if real is None else real + first
                    imaginary = second if imaginary is None else imaginary + second
                for part, value in enumerate((real, imaginary)):
                    at = component(part, 2 * chirality, i)
                    field[at] = value - kept * smooth[at]
                    smooth[at] = value

        @pl.when(sweep == 0)
        def _():
            pl.semaphore_wait(barrier, greeted)

        for order, (mu, axis) in enumerate(CROSSING):
            half = project(load_field, mu, -1)
            for part in range(2):
                for color in range(3):
                    outbox[sweep, 2 * order, part * 3 + color] = pack(
                        [half[0][color][part], half[1][color][part]], mu, False)
        for order, (mu, axis) in enumerate(CROSSING):
            half = project(load_field, mu, 1)
            packed = [
                tuple(pack([half[0][color][part], half[1][color][part]], mu, True) for part in range(2))
                for color in range(3)
            ]

            def face_link(part, row, column, order=order):
                return face_links[order, part, row * 3 + column]

            for row in range(3):
                pair = color_row(face_link, packed, row, True)
                for part in range(2):
                    outbox[sweep, 2 * order + 1, part * 3 + row] = pair[part]
        for order, (mu, axis) in enumerate(CROSSING):
            message(sweep, 2 * order, axis, -1).start()
            message(sweep, 2 * order + 1, axis, 1).start()

        @pl.when(sweep == 0)
        def _():
            loads[3].start()
            loads[4].wait()
            owner = [owners[i] for i in range(AGGS)]
            target = []
            for i in range(AGGS):
                rank = jnp.int32(0)
                for j in range(i):
                    rank = rank + jnp.where(owner[j] == owner[i], 1, 0)
                target.append(owner[i] * MOST + rank)
            lane_from = lax.broadcasted_iota(jnp.int32, (128, 128), 0)
            lane_to = lax.broadcasted_iota(jnp.int32, (128, 128), 1)
            slot_of = jnp.zeros((128, 128), jnp.int32)
            for i in range(AGGS):
                slot_of = jnp.where((lane_from // 4) % AGGS == i, target[i], slot_of)
            same_site = (lane_from // LY) * 4 + lane_from % 4 == lane_to % 16
            for part in range(slots // 8):
                placing[:, part * 128:(part + 1) * 128] = jnp.where(
                    same_site & (slot_of == lane_to // 16 + part * 8), 1.0, 0.0
                ).astype(BF16)
            for mu in range(4):
                for part in range(2):
                    for at in range(9):
                        links[mu, part, at] = links16[mu, part, at].astype(F32).reshape(2, 8, 128)

        started = False
        for mu in (HEIGHT, TIME, DEPTH, WIDTH):
            def link(part, row, column, mu=mu):
                return links[mu, part, row * 3 + column]

            for sign in (-1, 1):
                half = project(load_field, mu, sign)
                if sign < 0:
                    half = [[tuple(neighbour(value, mu, True) for value in pair) for pair in spin] for spin in half]
                for row in range(3):
                    moved = []
                    for spin in range(2):
                        pair = color_row(link, half[spin], row, sign > 0)
                        if sign > 0:
                            pair = tuple(neighbour(value, mu, False) for value in pair)
                        moved.append(pair)
                    for spin in range(4):
                        places = [component(part, spin, row) for part in range(2)]
                        base = tuple(acc[at] for at in places) if started else (0.0, 0.0)
                        if spin < 2:
                            total = add_phase(base, moved[spin], 0, 1)
                        else:
                            source, power = LOWER[mu][spin - 2]
                            total = add_phase(base, moved[source], power, sign)
                        for at, value in zip(places, total):
                            acc[at] = value
                started = True

        @pl.when(sweep == 1)
        def _():
            loads[3].wait()

            def widen(at, carry):
                for v in range(NV):
                    near32[at * NV + v] = near[at * NV + v].astype(F32).reshape(6, 8, 128)
                return carry

            lax.fori_loop(0, slots, widen, 0)

        for order, (mu, axis) in reversed(list(enumerate(CROSSING))):
            message(sweep, 2 * order, axis, -1).wait_recv()
            message(sweep, 2 * order + 1, axis, 1).wait_recv()

            def face_link(part, at_row, column, order=order):
                return face_links[order, part, at_row * 3 + column]

            for row in range(3):
                totals = [
                    [[acc[component(part, spin, row), side] for side in range(2)] for part in range(2)]
                    for spin in range(4)
                ]
                for sign in (-1, 1):
                    way = 2 * order + (0 if sign < 0 else 1)
                    if sign < 0:
                        packed = [
                            (inbox[sweep, way, color], inbox[sweep, way, 3 + color]) for color in range(3)
                        ]
                        pair = color_row(face_link, packed, row, False)
                    else:
                        pair = inbox[sweep, way, row], inbox[sweep, way, 3 + row]
                    spread = [unpack(value, mu, sign < 0) for value in pair]
                    for side in range(2):
                        if spread[0][0][side] is None:
                            continue
                        pieces = [(spread[0][spin][side], spread[1][spin][side]) for spin in range(2)]
                        for spin in range(4):
                            base = totals[spin][0][side], totals[spin][1][side]
                            if spin < 2:
                                total = add_phase(base, pieces[spin], 0, 1)
                            else:
                                source, power = LOWER[mu][spin - 2]
                                total = add_phase(base, pieces[source], power, sign)
                            totals[spin][0][side], totals[spin][1][side] = total
                for spin in range(4):
                    for part in range(2):
                        for side in range(2):
                            acc[component(part, spin, row), side] = totals[spin][part][side]
        return carry

    lax.fori_loop(0, SWEEPS, body, 0)

    for part in range(2):
        for color in range(3):
            for spin in range(4):
                value = HOPPING * acc[component(part, spin, color)]
                for side in range(2):
                    at = ((part * 3 + color) * 2 + side) * 4 + spin
                    tiles[at * 8:(at + 1) * 8, :] = value[side]
    rows = jnp.concatenate([tiles[pl.ds(r, 48, stride=8), :] for r in range(8)], axis=0).astype(BF16)
    mine = me["xy"]

    def parcel(owner):
        return pltpu.make_async_remote_copy(
            src_ref=parcels.at[owner],
            dst_ref=arrived.at[mine],
            send_sem=parcel_send.at[owner],
            recv_sem=parcel_recv.at[mine],
            device_id={"xy": owner},
            device_id_type=MESH,
        )

    placed = jnp.dot(rows, placing[...], preferred_element_type=F32)
    lane = lax.broadcasted_iota(jnp.int32, (48, 128), 1) // 16
    flags = {step: jnp.where((lane & step) != 0, 1.0, 0.0).astype(BF16) for step in (1, 2, 4)}
    for part in range(slots // 8):
        parts = [placed[r * 48:(r + 1) * 48, part * 128:(part + 1) * 128].astype(BF16) for r in range(8)]
        for step in (4, 2, 1):
            for r in range(8):
                if r & step:
                    continue
                first, second = parts[r], parts[r + step]
                odd = flags[step] > 0
                parts[r] = jnp.where(odd, roll(second, step * 16, 1), first)
                parts[r + step] = jnp.where(odd, second, roll(first, -step * 16, 1))
        for r in range(8):
            slot = part * 8 + r
            parcels[slot // MOST, slot % MOST] = parts[r]
    for turn in sorted(range(1, groups), key=lambda o: -min(o, groups - o)):
        parcel(lax.rem(mine + turn, groups)).start()

    for sweep in range(SWEEPS):
        for order, (mu, axis) in enumerate(CROSSING):
            message(sweep, 2 * order, axis, -1).wait_send()
            message(sweep, 2 * order + 1, axis, 1).wait_send()
    def contract(index, carry):
        pair = index // 2
        away = jnp.where(pair == 2, groups // 2 - 1, jnp.where(pair == 3, groups // 2 - 2, pair))
        chip = lax.rem(mine // 2 + away, groups // 2)
        source = chip * 2 + lax.rem(mine + index, 2)

        @pl.when(index > 0)
        def _():
            pltpu.make_async_remote_copy(
                src_ref=parcels.at[source],
                dst_ref=arrived.at[source],
                send_sem=parcel_send.at[source],
                recv_sem=parcel_recv.at[source],
                device_id={"xy": source},
                device_id_type=MESH,
            ).wait_recv()

        @pl.when(index == 0)
        def _():
            arrived[mine] = parcels[mine]

        for m in range(MOST):
            slot = source * MOST + m
            tile = arrived[source, m].astype(F32).reshape(6, 8, 128)
            turned = jnp.concatenate([tile[3:], -tile[:3]], axis=0)
            for v in range(NV):
                vector = near32[slot * NV + v]
                for part, other in enumerate((tile, turned)):
                    total = jnp.sum(jnp.sum(vector * other, axis=0), axis=1, keepdims=True)
                    sums[v * 2 + part] = jnp.where(lane8 == slot, total, sums[v * 2 + part])
        return carry

    lax.fori_loop(0, groups, contract, 0)
    for turn in range(1, groups):
        parcel(lax.rem(mine + turn, groups)).wait_send()


def finish(smooth, sums, smoothed, coarse, staged, sems):
    first = pltpu.make_async_copy(smooth, smoothed, sems.at[0])
    first.start()
    slots = coarse.shape[-1]
    total = sums[...]
    total = total + roll(total, 4, 1)
    total = total + roll(total, -1, 1)
    total = total.reshape(NV, 2, 8, 128)
    for chirality in range(2):
        staged[chirality] = total[:, :, 2 * chirality, :slots]
    second = pltpu.make_async_copy(staged, coarse, sems.at[1])
    second.start()
    first.wait()
    second.wait()


def shards(right_side, links, clover_inverse, near_null, owners):
    groups = lax.axis_size("xy")
    slots = groups * MOST
    near = jnp.transpose(near_null[0, 0, 0], (0, 1, 2, 4, 3, 5)).reshape(slots, NV, 2, 3, 4, 2, 128)
    near = jnp.transpose(near, (0, 1, 2, 3, 5, 4, 6)).reshape(slots * NV, 48, 128)
    anywhere = pl.BlockSpec(memory_space=pl.ANY)
    vmem = pltpu.VMEM
    inside = pl.BlockSpec(memory_space=vmem)
    operands = [
        pltpu.with_memory_space_constraint(value, pltpu.HBM)
        for value in (
            right_side.reshape(24, 2, 8, 128),
            links.reshape(4, 2, 9, 16, 128),
            clover_inverse.reshape(2, 2, 36, 16, 128),
            near,
            owners.reshape(-1),
        )
    ]
    smooth, sums = pl.pallas_call(
        kernel,
        out_shape=(vmem((24, 2, 8, 128), F32), vmem((NV * 2, 8, 128), F32)),
        in_specs=[anywhere] * 5,
        out_specs=(inside, inside),
        scratch_shapes=[
            vmem((24, 2, 8, 128), F32),
            vmem((4, 2, 9, 16, 128), BF16),
            vmem((2, 2, 36, 16, 128), BF16),
            vmem((slots * NV, 48, 128), BF16),
            vmem((slots * NV, 6, 8, 128), F32),
            pltpu.SMEM((AGGS,), jnp.int32),
            vmem((4, 2, 9, 2, 8, 128), F32),
            vmem((3, 2, 9, 8, 128), F32),
            vmem((24, 2, 8, 128), F32),
            vmem((24, 2, 8, 128), F32),
            vmem((SWEEPS, 6, 6, 8, 128), F32),
            vmem((SWEEPS, 6, 6, 8, 128), F32),
            vmem((384, 128), F32),
            vmem((128, slots * 16), BF16),
            vmem((groups, MOST, 48, 128), BF16),
            vmem((groups, MOST, 48, 128), BF16),
            pltpu.SemaphoreType.DMA((5,)),
            pltpu.SemaphoreType.DMA((SWEEPS, 6)),
            pltpu.SemaphoreType.DMA((SWEEPS, 6)),
            pltpu.SemaphoreType.DMA((groups,)),
            pltpu.SemaphoreType.DMA((groups,)),
        ],
        compiler_params=pltpu.CompilerParams(
            collective_id=0, has_side_effects=True, vmem_limit_bytes=32 * 1024 * 1024
        ),
        name="smooth_and_restrict",
    )(*operands)
    smoothed, coarse = pl.pallas_call(
        finish,
        out_shape=(
            jax.ShapeDtypeStruct((24, 2, 8, 128), F32),
            jax.ShapeDtypeStruct((2, NV, 2, slots), F32),
        ),
        in_specs=[anywhere, inside],
        out_specs=(anywhere, anywhere),
        scratch_shapes=[vmem((2, NV, 2, slots), F32), pltpu.SemaphoreType.DMA((2,))],
        compiler_params=pltpu.CompilerParams(vmem_limit_bytes=32 * 1024 * 1024),
        name="finish",
    )(smooth, sums)
    coarse = jnp.transpose(coarse, (3, 0, 2, 1))[None, None, None]
    return smoothed.reshape(2, 4, 3, 4, 4, 128), coarse


def solution(mesh):
    placed = (
        P(None, None, None, "ta", "gz", "xy"),
        P(None, None, None, None, "ta", "gz", "xy"),
        P(None, None, None, None, "ta", "gz", "xy"),
        P("ta", "gz", "xy", None, None, None, None, None, None),
        P("ta", "gz", "xy", None),
    )
    return jax.shard_map(
        shards,
        mesh=mesh,
        in_specs=placed,
        out_specs=(
            P(None, None, None, "ta", "gz", "xy"),
            P("ta", "gz", "xy", None, None, None, None),
        ),
        check_vma=False,
    )
```

```python
import jax
import jax.numpy as jnp
from jax import lax
from jax.experimental import pallas as pl
from jax.experimental.pallas import tpu as pltpu
from jax.sharding import PartitionSpec as P

LY = 32
SWEEPS = 3
MOST = 2
AGGS = 8
NV = 12
HOPPING = 0.13
F32 = jnp.float32
BF16 = jnp.bfloat16
MESH = pl.DeviceIdType.MESH
WIDTH, HEIGHT, DEPTH, TIME = range(4)
CROSSING = ((TIME, "ta"), (DEPTH, "gz"), (WIDTH, "xy"))
UPPER = {
    WIDTH: ((1, 3), (0, 3)),
    HEIGHT: ((1, 2), (0, 0)),
    DEPTH: ((0, 3), (1, 1)),
    TIME: ((0, 0), (1, 0)),
}
LOWER = {
    WIDTH: ((1, 1), (0, 1)),
    HEIGHT: ((1, 0), (0, 2)),
    DEPTH: ((0, 1), (1, 3)),
    TIME: ((0, 0), (1, 0)),
}


def roll(value, shift, axis):
    size = value.shape[axis]
    shift = shift % size
    return value if shift == 0 else pltpu.roll(value, shift, axis)


def add_phase(base, pair, power, sign):
    if sign < 0:
        power = power + 2
    real, imaginary = pair
    turned = ((real, 1), (imaginary, 1)), ((imaginary, -1), (real, 1)), ((real, -1), (imaginary, -1)), ((imaginary, 1), (real, -1))
    out = []
    for part, (value, factor) in zip(base, turned[power % 4]):
        out.append(part + value if factor > 0 else part - value)
    return tuple(out)


def project(load, mu, sign):
    half = []
    for spin in range(2):
        source, power = UPPER[mu][spin]
        half.append([
            add_phase(load(spin, color), load(2 + source, color), power, sign)
            for color in range(3)
        ])
    return half


def color_row(link, vector, row, adjoint):
    real = imaginary = None
    for column in range(3):
        at = (column, row) if adjoint else (row, column)
        link_real, link_imaginary = link(0, *at), link(1, *at)
        vector_real, vector_imaginary = vector[column]
        first, second = link_real * vector_real, link_real * vector_imaginary
        third, fourth = link_imaginary * vector_imaginary, link_imaginary * vector_real
        if adjoint:
            first, second = first + third, second - fourth
        else:
            first, second = first - third, second + fourth
        real = first if real is None else real + first
        imaginary = second if imaginary is None else imaginary + second
    return real, imaginary


def kernel(rs_hbm, links_hbm, clover_hbm, near_hbm, owners_hbm, smooth, sums,
           rs, links16, clover, near, owners, links, face_links, field, acc,
           outbox, inbox, tiles, placing, parcels, arrived,
           load_sem, send_sem, recv_sem, parcel_send, parcel_recv):
    groups = lax.axis_size("xy")
    slots = groups * MOST
    me = {axis: lax.axis_index(axis) for axis in ("ta", "gz", "xy")}

    def shifted(axis, offset):
        size = lax.axis_size(axis)
        return lax.rem(me[axis] + (offset + size), size)

    loads = [
        pltpu.make_async_copy(source, target, load_sem.at[i])
        for i, (source, target) in enumerate(
            ((links_hbm, links16), (rs_hbm, rs), (clover_hbm, clover), (near_hbm, near), (owners_hbm, owners))
        )
    ]
    for copy in loads[:3] + loads[4:]:
        copy.start()

    barrier = pltpu.get_barrier_semaphore()
    greeted = 0
    for axis in ("ta", "gz"):
        for offset in (1, -1):
            pl.semaphore_signal(barrier, inc=1, device_id={axis: shifted(axis, offset)}, device_id_type=MESH)
            greeted += 1
    for offset in range(1, groups):
        pl.semaphore_signal(barrier, inc=1, device_id={"xy": shifted("xy", offset)}, device_id_type=MESH)
        greeted += 1

    row8 = lax.broadcasted_iota(jnp.int32, (8, 128), 0)
    lane8 = lax.broadcasted_iota(jnp.int32, (8, 128), 1)
    upper_rows = row8 >= 4
    depth_at = row8 % 4
    width_at = lane8 // LY
    height_at = lane8 % LY

    def pack(values, mu, high):
        if mu == TIME:
            if high:
                return jnp.where(upper_rows, values[1][1], roll(values[0][1], 4, 0))
            return jnp.where(upper_rows, roll(values[1][0], 4, 0), values[0][0])
        axis, unit, at = (0, 1, depth_at) if mu == DEPTH else (1, LY, width_at)
        face = 3 if high else 0
        out = None
        for index in range(4):
            piece = roll(values[index // 2][index % 2], (index - face) * unit, axis)
            out = piece if out is None else jnp.where(at == index, piece, out)
        return out

    def unpack(packed, mu, high):
        if mu == TIME:
            if high:
                return [
                    (None, jnp.where(upper_rows, roll(packed, 4 * (1 - spin), 0), 0.0))
                    for spin in range(2)
                ]
            return [
                (jnp.where(upper_rows, 0.0, roll(packed, 4 * spin, 0)), None)
                for spin in range(2)
            ]
        axis, unit, at = (0, 1, depth_at) if mu == DEPTH else (1, LY, width_at)
        face = 3 if high else 0
        pieces = [
            jnp.where(at == face, roll(packed, (face - index) * unit, axis), 0.0)
            for index in range(4)
        ]
        return [(pieces[2 * spin], pieces[2 * spin + 1]) for spin in range(2)]

    def neighbour(value, mu, ahead):
        if mu == HEIGHT:
            step = -1 if ahead else 1
            edge = height_at == (LY - 1 if ahead else 0)
            return jnp.where(edge[None], roll(value, -step * (LY - 1), 2), roll(value, step, 2))
        if mu == TIME:
            turned = roll(value, 4, 1)
            if ahead:
                first = jnp.where(upper_rows, turned[1], turned[0])
                second = jnp.where(upper_rows, 0.0, turned[1])
            else:
                first = jnp.where(upper_rows, turned[0], 0.0)
                second = jnp.where(upper_rows, turned[1], turned[0])
            return jnp.stack([first, second])
        axis, unit, at = (1, 1, depth_at) if mu == DEPTH else (2, LY, width_at)
        edge = at == (3 if ahead else 0)
        return jnp.where(edge[None], 0.0, roll(value, -unit if ahead else unit, axis))

    def component(part, spin, color):
        return (part * 4 + spin) * 3 + color

    def load_field(spin, color):
        return field[component(0, spin, color)], field[component(1, spin, color)]

    def message(sweep, way, axis, offset):
        return pltpu.make_async_remote_copy(
            src_ref=outbox.at[sweep, way],
            dst_ref=inbox.at[sweep, way],
            send_sem=send_sem.at[sweep, way],
            recv_sem=recv_sem.at[sweep, way],
            device_id={axis: shifted(axis, offset)},
            device_id_type=MESH,
        )

    acc[...] = jnp.zeros(acc.shape, F32)
    smooth[...] = jnp.zeros(smooth.shape, F32)
    sums[...] = jnp.zeros(sums.shape, F32)

    loads[0].wait()
    for order, (mu, _) in enumerate(CROSSING):
        for part in range(2):
            for at in range(9):
                value = links16[mu, part, at].astype(F32).reshape(2, 8, 128)
                face_links[order, part, at] = pack([value, value], mu, True)
    loads[1].wait()
    loads[2].wait()

    def body(sweep, carry):
        kept = jnp.where(sweep == SWEEPS - 1, 1.0, 0.0)
        for chirality in range(2):
            vector = [
                [rs[component(part, 2 * chirality, j)] + HOPPING * acc[component(part, 2 * chirality, j)]
                 for part in range(2)]
                for j in range(6)
            ]
            for i in range(6):
                real = imaginary = None
                for j in range(6):
                    block_real = clover[chirality, 0, i * 6 + j].astype(F32).reshape(2, 8, 128)
                    block_imaginary = clover[chirality, 1, i * 6 + j].astype(F32).reshape(2, 8, 128)
                    first = block_real * vector[j][0] - block_imaginary * vector[j][1]
                    second = block_real * vector[j][1] + block_imaginary * vector[j][0]
                    real = first if real is None else real + first
                    imaginary = second if imaginary is None else imaginary + second
                for part, value in enumerate((real, imaginary)):
                    at = component(part, 2 * chirality, i)
                    field[at] = value - kept * smooth[at]
                    smooth[at] = value

        @pl.when(sweep == 0)
        def _():
            pl.semaphore_wait(barrier, greeted)

        for order, (mu, axis) in enumerate(CROSSING):
            half = project(load_field, mu, -1)
            for part in range(2):
                for color in range(3):
                    outbox[sweep, 2 * order, part * 3 + color] = pack(
                        [half[0][color][part], half[1][color][part]], mu, False)
        for order, (mu, axis) in enumerate(CROSSING):
            half = project(load_field, mu, 1)
            packed = [
                tuple(pack([half[0][color][part], half[1][color][part]], mu, True) for part in range(2))
                for color in range(3)
            ]

            def face_link(part, row, column, order=order):
                return face_links[order, part, row * 3 + column]

            for row in range(3):
                pair = color_row(face_link, packed, row, True)
                for part in range(2):
                    outbox[sweep, 2 * order + 1, part * 3 + row] = pair[part]
        for order, (mu, axis) in enumerate(CROSSING):
            message(sweep, 2 * order, axis, -1).start()
            message(sweep, 2 * order + 1, axis, 1).start()

        @pl.when(sweep == 0)
        def _():
            loads[3].start()
            loads[4].wait()
            owner = [owners[i] for i in range(AGGS)]
            target = []
            for i in range(AGGS):
                rank = jnp.int32(0)
                for j in range(i):
                    rank = rank + jnp.where(owner[j] == owner[i], 1, 0)
                target.append(owner[i] * MOST + rank)
            lane_from = lax.broadcasted_iota(jnp.int32, (128, 128), 0)
            lane_to = lax.broadcasted_iota(jnp.int32, (128, 128), 1)
            slot_of = jnp.zeros((128, 128), jnp.int32)
            for i in range(AGGS):
                slot_of = jnp.where((lane_from // 4) % AGGS == i, target[i], slot_of)
            same_site = (lane_from // LY) * 4 + lane_from % 4 == lane_to % 16
            for part in range(slots // 8):
                placing[:, part * 128:(part + 1) * 128] = jnp.where(
                    same_site & (slot_of == lane_to // 16 + part * 8), 1.0, 0.0
                ).astype(BF16)
            for mu in range(4):
                for part in range(2):
                    for at in range(9):
                        links[mu, part, at] = links16[mu, part, at].astype(F32).reshape(2, 8, 128)

        started = False
        for mu in (HEIGHT, TIME, DEPTH, WIDTH):
            def link(part, row, column, mu=mu):
                return links[mu, part, row * 3 + column]

            for sign in (-1, 1):
                half = project(load_field, mu, sign)
                if sign < 0:
                    half = [[tuple(neighbour(value, mu, True) for value in pair) for pair in spin] for spin in half]
                for row in range(3):
                    moved = []
                    for spin in range(2):
                        pair = color_row(link, half[spin], row, sign > 0)
                        if sign > 0:
                            pair = tuple(neighbour(value, mu, False) for value in pair)
                        moved.append(pair)
                    for spin in range(4):
                        places = [component(part, spin, row) for part in range(2)]
                        base = tuple(acc[at] for at in places) if started else (0.0, 0.0)
                        if spin < 2:
                            total = add_phase(base, moved[spin], 0, 1)
                        else:
                            source, power = LOWER[mu][spin - 2]
                            total = add_phase(base, moved[source], power, sign)
                        for at, value in zip(places, total):
                            acc[at] = value
                started = True

        for order, (mu, axis) in reversed(list(enumerate(CROSSING))):
            message(sweep, 2 * order, axis, -1).wait_recv()
            message(sweep, 2 * order + 1, axis, 1).wait_recv()

            def face_link(part, at_row, column, order=order):
                return face_links[order, part, at_row * 3 + column]

            for row in range(3):
                totals = [
                    [[acc[component(part, spin, row), side] for side in range(2)] for part in range(2)]
                    for spin in range(4)
                ]
                for sign in (-1, 1):
                    way = 2 * order + (0 if sign < 0 else 1)
                    if sign < 0:
                        packed = [
                            (inbox[sweep, way, color], inbox[sweep, way, 3 + color]) for color in range(3)
                        ]
                        pair = color_row(face_link, packed, row, False)
                    else:
                        pair = inbox[sweep, way, row], inbox[sweep, way, 3 + row]
                    spread = [unpack(value, mu, sign < 0) for value in pair]
                    for side in range(2):
                        if spread[0][0][side] is None:
                            continue
                        pieces = [(spread[0][spin][side], spread[1][spin][side]) for spin in range(2)]
                        for spin in range(4):
                            base = totals[spin][0][side], totals[spin][1][side]
                            if spin < 2:
                                total = add_phase(base, pieces[spin], 0, 1)
                            else:
                                source, power = LOWER[mu][spin - 2]
                                total = add_phase(base, pieces[source], power, sign)
                            totals[spin][0][side], totals[spin][1][side] = total
                for spin in range(4):
                    for part in range(2):
                        for side in range(2):
                            acc[component(part, spin, row), side] = totals[spin][part][side]
        return carry

    lax.fori_loop(0, SWEEPS, body, 0)

    for part in range(2):
        for color in range(3):
            for spin in range(4):
                value = HOPPING * acc[component(part, spin, color)]
                for side in range(2):
                    at = ((part * 3 + color) * 2 + side) * 4 + spin
                    tiles[at * 8:(at + 1) * 8, :] = value[side]
    rows = jnp.concatenate([tiles[pl.ds(r, 48, stride=8), :] for r in range(8)], axis=0).astype(BF16)
    mine = me["xy"]

    def parcel(owner):
        return pltpu.make_async_remote_copy(
            src_ref=parcels.at[owner],
            dst_ref=arrived.at[mine],
            send_sem=parcel_send.at[owner],
            recv_sem=parcel_recv.at[mine],
            device_id={"xy": owner},
            device_id_type=MESH,
        )

    placed = jnp.dot(rows, placing[...], preferred_element_type=F32)
    lane = lax.broadcasted_iota(jnp.int32, (48, 128), 1) // 16
    flags = {step: jnp.where((lane & step) != 0, 1.0, 0.0).astype(BF16) for step in (1, 2, 4)}
    for part in range(slots // 8):
        parts = [placed[r * 48:(r + 1) * 48, part * 128:(part + 1) * 128].astype(BF16) for r in range(8)]
        for step in (4, 2, 1):
            for r in range(8):
                if r & step:
                    continue
                first, second = parts[r], parts[r + step]
                odd = flags[step] > 0
                parts[r] = jnp.where(odd, roll(second, step * 16, 1), first)
                parts[r + step] = jnp.where(odd, second, roll(first, -step * 16, 1))
        for r in range(8):
            slot = part * 8 + r
            parcels[slot // MOST, slot % MOST] = parts[r]
    for turn in sorted(range(1, groups), key=lambda o: -min(o, groups - o)):
        parcel(lax.rem(mine + turn, groups)).start()

    for sweep in range(SWEEPS):
        for order, (mu, axis) in enumerate(CROSSING):
            message(sweep, 2 * order, axis, -1).wait_send()
            message(sweep, 2 * order + 1, axis, 1).wait_send()
    loads[3].wait()

    def contract(index, carry):
        pair = index // 2
        away = jnp.where(pair == 2, groups // 2 - 1, jnp.where(pair == 3, groups // 2 - 2, pair))
        chip = lax.rem(mine // 2 + away, groups // 2)
        source = chip * 2 + lax.rem(mine + index, 2)

        @pl.when(index > 0)
        def _():
            pltpu.make_async_remote_copy(
                src_ref=parcels.at[source],
                dst_ref=arrived.at[source],
                send_sem=parcel_send.at[source],
                recv_sem=parcel_recv.at[source],
                device_id={"xy": source},
                device_id_type=MESH,
            ).wait_recv()

        @pl.when(index == 0)
        def _():
            arrived[mine] = parcels[mine]

        for m in range(MOST):
            slot = source * MOST + m
            tile = arrived[source, m].astype(F32).reshape(6, 8, 128)
            turned = jnp.concatenate([tile[3:], -tile[:3]], axis=0)
            for v in range(NV):
                vector = near[slot * NV + v].astype(F32).reshape(6, 8, 128)
                real, imaginary = (jnp.sum(vector * other, axis=0) for other in (tile, turned))
                both = jnp.where(upper_rows, imaginary, real)
                both = both + roll(jnp.where(upper_rows, real, imaginary), 4, 0)
                total = jnp.sum(both, axis=1, keepdims=True)
                sums[v] = jnp.where(lane8 == slot, total, sums[v])
        return carry

    lax.fori_loop(0, groups, contract, 0)
    for turn in range(1, groups):
        parcel(lax.rem(mine + turn, groups)).wait_send()


def finish(smooth, sums, smoothed, coarse, staged, sems):
    first = pltpu.make_async_copy(smooth, smoothed, sems.at[0])
    first.start()
    slots = coarse.shape[-1]
    total = sums[...]
    total = total + roll(total, -1, 1)
    for chirality in range(2):
        for part in range(2):
            staged[chirality, :, part] = total[:, 4 * part + 2 * chirality, :slots]
    second = pltpu.make_async_copy(staged, coarse, sems.at[1])
    second.start()
    first.wait()
    second.wait()


def shards(right_side, links, clover_inverse, near_null, owners):
    groups = lax.axis_size("xy")
    slots = groups * MOST
    near = jnp.transpose(near_null[0, 0, 0], (0, 1, 2, 4, 3, 5)).reshape(slots, NV, 2, 3, 4, 2, 128)
    near = jnp.transpose(near, (0, 1, 2, 3, 5, 4, 6)).reshape(slots * NV, 48, 128)
    anywhere = pl.BlockSpec(memory_space=pl.ANY)
    vmem = pltpu.VMEM
    inside = pl.BlockSpec(memory_space=vmem)
    operands = [
        pltpu.with_memory_space_constraint(value, pltpu.HBM)
        for value in (
            right_side.reshape(24, 2, 8, 128),
            links.reshape(4, 2, 9, 16, 128),
            clover_inverse.reshape(2, 2, 36, 16, 128),
            near,
            owners.reshape(-1),
        )
    ]
    smooth, sums = pl.pallas_call(
        kernel,
        out_shape=(vmem((24, 2, 8, 128), F32), vmem((NV, 8, 128), F32)),
        in_specs=[anywhere] * 5,
        out_specs=(inside, inside),
        scratch_shapes=[
            vmem((24, 2, 8, 128), F32),
            vmem((4, 2, 9, 16, 128), BF16),
            vmem((2, 2, 36, 16, 128), BF16),
            vmem((slots * NV, 48, 128), BF16),
            pltpu.SMEM((AGGS,), jnp.int32),
            vmem((4, 2, 9, 2, 8, 128), F32),
            vmem((3, 2, 9, 8, 128), F32),
            vmem((24, 2, 8, 128), F32),
            vmem((24, 2, 8, 128), F32),
            vmem((SWEEPS, 6, 6, 8, 128), F32),
            vmem((SWEEPS, 6, 6, 8, 128), F32),
            vmem((384, 128), F32),
            vmem((128, slots * 16), BF16),
            vmem((groups, MOST, 48, 128), BF16),
            vmem((groups, MOST, 48, 128), BF16),
            pltpu.SemaphoreType.DMA((5,)),
            pltpu.SemaphoreType.DMA((SWEEPS, 6)),
            pltpu.SemaphoreType.DMA((SWEEPS, 6)),
            pltpu.SemaphoreType.DMA((groups,)),
            pltpu.SemaphoreType.DMA((groups,)),
        ],
        compiler_params=pltpu.CompilerParams(
            collective_id=0, has_side_effects=True, vmem_limit_bytes=32 * 1024 * 1024
        ),
        name="smooth_and_restrict",
    )(*operands)
    smoothed, coarse = pl.pallas_call(
        finish,
        out_shape=(
            jax.ShapeDtypeStruct((24, 2, 8, 128), F32),
            jax.ShapeDtypeStruct((2, NV, 2, slots), F32),
        ),
        in_specs=[anywhere, inside],
        out_specs=(anywhere, anywhere),
        scratch_shapes=[vmem((2, NV, 2, slots), F32), pltpu.SemaphoreType.DMA((2,))],
        compiler_params=pltpu.CompilerParams(vmem_limit_bytes=32 * 1024 * 1024),
        name="finish",
    )(smooth, sums)
    coarse = jnp.transpose(coarse, (3, 0, 2, 1))[None, None, None]
    return smoothed.reshape(2, 4, 3, 4, 4, 128), coarse


def solution(mesh):
    placed = (
        P(None, None, None, "ta", "gz", "xy"),
        P(None, None, None, None, "ta", "gz", "xy"),
        P(None, None, None, None, "ta", "gz", "xy"),
        P("ta", "gz", "xy", None, None, None, None, None, None),
        P("ta", "gz", "xy", None),
    )
    return jax.shard_map(
        shards,
        mesh=mesh,
        in_specs=placed,
        out_specs=(
            P(None, None, None, "ta", "gz", "xy"),
            P("ta", "gz", "xy", None, None, None, None),
        ),
        check_vma=False,
    )
```

```python
import jax
import jax.numpy as jnp
from jax import lax
from jax.experimental import pallas as pl
from jax.experimental.pallas import tpu as pltpu
from jax.sharding import PartitionSpec as P

LY = 32
SWEEPS = 3
MOST = 2
AGGS = 8
NV = 12
HOPPING = 0.13
F32 = jnp.float32
BF16 = jnp.bfloat16
MESH = pl.DeviceIdType.MESH
WIDTH, HEIGHT, DEPTH, TIME = range(4)
CROSSING = ((TIME, "ta"), (DEPTH, "gz"), (WIDTH, "xy"))
UPPER = {
    WIDTH: ((1, 3), (0, 3)),
    HEIGHT: ((1, 2), (0, 0)),
    DEPTH: ((0, 3), (1, 1)),
    TIME: ((0, 0), (1, 0)),
}
LOWER = {
    WIDTH: ((1, 1), (0, 1)),
    HEIGHT: ((1, 0), (0, 2)),
    DEPTH: ((0, 1), (1, 3)),
    TIME: ((0, 0), (1, 0)),
}


def roll(value, shift, axis):
    size = value.shape[axis]
    shift = shift % size
    return value if shift == 0 else pltpu.roll(value, shift, axis)


def add_phase(base, pair, power, sign):
    if sign < 0:
        power = power + 2
    real, imaginary = pair
    turned = ((real, 1), (imaginary, 1)), ((imaginary, -1), (real, 1)), ((real, -1), (imaginary, -1)), ((imaginary, 1), (real, -1))
    out = []
    for part, (value, factor) in zip(base, turned[power % 4]):
        out.append(part + value if factor > 0 else part - value)
    return tuple(out)


def project(load, mu, sign):
    half = []
    for spin in range(2):
        source, power = UPPER[mu][spin]
        half.append([
            add_phase(load(spin, color), load(2 + source, color), power, sign)
            for color in range(3)
        ])
    return half


def color_row(link, vector, row, adjoint):
    real = imaginary = None
    for column in range(3):
        at = (column, row) if adjoint else (row, column)
        link_real, link_imaginary = link(0, *at), link(1, *at)
        vector_real, vector_imaginary = vector[column]
        first, second = link_real * vector_real, link_real * vector_imaginary
        third, fourth = link_imaginary * vector_imaginary, link_imaginary * vector_real
        if adjoint:
            first, second = first + third, second - fourth
        else:
            first, second = first - third, second + fourth
        real = first if real is None else real + first
        imaginary = second if imaginary is None else imaginary + second
    return real, imaginary


def kernel(rs_hbm, links_hbm, clover_hbm, near_hbm, owners_hbm, smooth, sums,
           rs, links16, clover, near, owners, links, face_links, field, hops,
           outbox, inbox, placing, parcels, arrived,
           load_sem, send_sem, recv_sem, parcel_send, parcel_recv):
    groups = lax.axis_size("xy")
    slots = groups * MOST
    me = {axis: lax.axis_index(axis) for axis in ("ta", "gz", "xy")}

    def shifted(axis, offset):
        size = lax.axis_size(axis)
        return lax.rem(me[axis] + (offset + size), size)

    loads = [
        pltpu.make_async_copy(source, target, load_sem.at[i])
        for i, (source, target) in enumerate(
            ((links_hbm, links16), (rs_hbm, rs), (clover_hbm, clover), (near_hbm, near), (owners_hbm, owners))
        )
    ]
    for copy in loads[:3] + loads[4:]:
        copy.start()

    barrier = pltpu.get_barrier_semaphore()
    greeted = 0
    for axis in ("ta", "gz"):
        for offset in (1, -1):
            pl.semaphore_signal(barrier, inc=1, device_id={axis: shifted(axis, offset)}, device_id_type=MESH)
            greeted += 1
    for offset in range(1, groups):
        pl.semaphore_signal(barrier, inc=1, device_id={"xy": shifted("xy", offset)}, device_id_type=MESH)
        greeted += 1

    row8 = lax.broadcasted_iota(jnp.int32, (8, 128), 0)
    lane8 = lax.broadcasted_iota(jnp.int32, (8, 128), 1)
    upper_rows = row8 >= 4
    depth_at = row8 % 4
    width_at = lane8 // LY
    height_at = lane8 % LY

    def pack(values, mu, high):
        if mu == TIME:
            if high:
                return jnp.where(upper_rows, values[1][1], roll(values[0][1], 4, 0))
            return jnp.where(upper_rows, roll(values[1][0], 4, 0), values[0][0])
        axis, unit, at = (0, 1, depth_at) if mu == DEPTH else (1, LY, width_at)
        face = 3 if high else 0
        out = None
        for index in range(4):
            piece = roll(values[index // 2][index % 2], (index - face) * unit, axis)
            out = piece if out is None else jnp.where(at == index, piece, out)
        return out

    def unpack(packed, mu, high):
        if mu == TIME:
            if high:
                return [
                    (None, jnp.where(upper_rows, roll(packed, 4 * (1 - spin), 0), 0.0))
                    for spin in range(2)
                ]
            return [
                (jnp.where(upper_rows, 0.0, roll(packed, 4 * spin, 0)), None)
                for spin in range(2)
            ]
        axis, unit, at = (0, 1, depth_at) if mu == DEPTH else (1, LY, width_at)
        face = 3 if high else 0
        pieces = [
            jnp.where(at == face, roll(packed, (face - index) * unit, axis), 0.0)
            for index in range(4)
        ]
        return [(pieces[2 * spin], pieces[2 * spin + 1]) for spin in range(2)]

    def neighbour(value, mu, ahead):
        if mu == HEIGHT:
            step = -1 if ahead else 1
            edge = height_at == (LY - 1 if ahead else 0)
            return jnp.where(edge[None], roll(value, -step * (LY - 1), 2), roll(value, step, 2))
        if mu == TIME:
            turned = roll(value, 4, 1)
            if ahead:
                first = jnp.where(upper_rows, turned[1], turned[0])
                second = jnp.where(upper_rows, 0.0, turned[1])
            else:
                first = jnp.where(upper_rows, turned[0], 0.0)
                second = jnp.where(upper_rows, turned[1], turned[0])
            return jnp.stack([first, second])
        axis, unit, at = (1, 1, depth_at) if mu == DEPTH else (2, LY, width_at)
        edge = at == (3 if ahead else 0)
        return jnp.where(edge[None], 0.0, roll(value, -unit if ahead else unit, axis))

    def component(part, spin, color):
        return (part * 4 + spin) * 3 + color

    def load_field(spin, color):
        return field[component(0, spin, color)], field[component(1, spin, color)]

    def hop_rows(part, spin, color, side):
        at = ((part * 3 + color) * 2 + side) * 4 + spin
        return slice(at * 8, (at + 1) * 8)

    def load_hop(part, spin, color):
        return jnp.stack([hops[hop_rows(part, spin, color, side), :] for side in range(2)])

    def store_hop(part, spin, color, value):
        for side in range(2):
            hops[hop_rows(part, spin, color, side), :] = value[side]

    def message(sweep, way, axis, offset):
        return pltpu.make_async_remote_copy(
            src_ref=outbox.at[sweep, way],
            dst_ref=inbox.at[sweep, way],
            send_sem=send_sem.at[sweep, way],
            recv_sem=recv_sem.at[sweep, way],
            device_id={axis: shifted(axis, offset)},
            device_id_type=MESH,
        )

    hops[...] = jnp.zeros(hops.shape, F32)
    smooth[...] = jnp.zeros(smooth.shape, F32)
    sums[...] = jnp.zeros(sums.shape, F32)

    loads[0].wait()
    for order, (mu, _) in enumerate(CROSSING):
        for part in range(2):
            for at in range(9):
                value = links16[mu, part, at].astype(F32).reshape(2, 8, 128)
                face_links[order, part, at] = pack([value, value], mu, True)
    loads[1].wait()
    loads[2].wait()

    def body(sweep, carry):
        kept = jnp.where(sweep == SWEEPS - 1, 1.0, 0.0)
        for chirality in range(2):
            vector = [
                [rs[component(part, 2 * chirality, j)] + HOPPING * load_hop(part, 2 * chirality + j // 3, j % 3)
                 for part in range(2)]
                for j in range(6)
            ]
            for i in range(6):
                real = imaginary = None
                for j in range(6):
                    block_real = clover[chirality, 0, i * 6 + j].astype(F32).reshape(2, 8, 128)
                    block_imaginary = clover[chirality, 1, i * 6 + j].astype(F32).reshape(2, 8, 128)
                    first = block_real * vector[j][0] - block_imaginary * vector[j][1]
                    second = block_real * vector[j][1] + block_imaginary * vector[j][0]
                    real = first if real is None else real + first
                    imaginary = second if imaginary is None else imaginary + second
                for part, value in enumerate((real, imaginary)):
                    at = component(part, 2 * chirality, i)
                    field[at] = value - kept * smooth[at]
                    smooth[at] = value

        @pl.when(sweep == 0)
        def _():
            pl.semaphore_wait(barrier, greeted)

        for order, (mu, axis) in enumerate(CROSSING):
            half = project(load_field, mu, -1)
            for part in range(2):
                for color in range(3):
                    outbox[sweep, 2 * order, part * 3 + color] = pack(
                        [half[0][color][part], half[1][color][part]], mu, False)
        for order, (mu, axis) in enumerate(CROSSING):
            half = project(load_field, mu, 1)
            packed = [
                tuple(pack([half[0][color][part], half[1][color][part]], mu, True) for part in range(2))
                for color in range(3)
            ]

            def face_link(part, row, column, order=order):
                return face_links[order, part, row * 3 + column]

            for row in range(3):
                pair = color_row(face_link, packed, row, True)
                for part in range(2):
                    outbox[sweep, 2 * order + 1, part * 3 + row] = pair[part]
        for order, (mu, axis) in enumerate(CROSSING):
            message(sweep, 2 * order, axis, -1).start()
            message(sweep, 2 * order + 1, axis, 1).start()

        @pl.when(sweep == 0)
        def _():
            loads[3].start()
            loads[4].wait()
            owner = [owners[i] for i in range(AGGS)]
            target = []
            for i in range(AGGS):
                rank = jnp.int32(0)
                for j in range(i):
                    rank = rank + jnp.where(owner[j] == owner[i], 1, 0)
                target.append(owner[i] * MOST + rank)
            lane_from = lax.broadcasted_iota(jnp.int32, (128, 128), 0)
            lane_to = lax.broadcasted_iota(jnp.int32, (128, 128), 1)
            slot_of = jnp.zeros((128, 128), jnp.int32)
            for i in range(AGGS):
                slot_of = jnp.where((lane_from // 4) % AGGS == i, target[i], slot_of)
            same_site = (lane_from // LY) * 4 + lane_from % 4 == lane_to % 16
            for part in range(slots // 8):
                placing[:, part * 128:(part + 1) * 128] = jnp.where(
                    same_site & (slot_of == lane_to // 16 + part * 8), 1.0, 0.0
                ).astype(BF16)
            for mu in range(4):
                for part in range(2):
                    for at in range(9):
                        links[mu, part, at] = links16[mu, part, at].astype(F32).reshape(2, 8, 128)

        started = False
        for mu in (HEIGHT, TIME, DEPTH, WIDTH):
            def link(part, row, column, mu=mu):
                return links[mu, part, row * 3 + column]

            for sign in (-1, 1):
                half = project(load_field, mu, sign)
                if sign < 0:
                    half = [[tuple(neighbour(value, mu, True) for value in pair) for pair in spin] for spin in half]
                for row in range(3):
                    moved = []
                    for spin in range(2):
                        pair = color_row(link, half[spin], row, sign > 0)
                        if sign > 0:
                            pair = tuple(neighbour(value, mu, False) for value in pair)
                        moved.append(pair)
                    for spin in range(4):
                        base = tuple(load_hop(part, spin, row) for part in range(2)) if started else (0.0, 0.0)
                        if spin < 2:
                            total = add_phase(base, moved[spin], 0, 1)
                        else:
                            source, power = LOWER[mu][spin - 2]
                            total = add_phase(base, moved[source], power, sign)
                        for part, value in enumerate(total):
                            store_hop(part, spin, row, value)
                started = True

        for order, (mu, axis) in reversed(list(enumerate(CROSSING))):
            message(sweep, 2 * order, axis, -1).wait_recv()
            message(sweep, 2 * order + 1, axis, 1).wait_recv()

            def face_link(part, at_row, column, order=order):
                return face_links[order, part, at_row * 3 + column]

            for row in range(3):
                totals = [
                    [[hops[hop_rows(part, spin, row, side), :] for side in range(2)] for part in range(2)]
                    for spin in range(4)
                ]
                for sign in (-1, 1):
                    way = 2 * order + (0 if sign < 0 else 1)
                    if sign < 0:
                        packed = [
                            (inbox[sweep, way, color], inbox[sweep, way, 3 + color]) for color in range(3)
                        ]
                        pair = color_row(face_link, packed, row, False)
                    else:
                        pair = inbox[sweep, way, row], inbox[sweep, way, 3 + row]
                    spread = [unpack(value, mu, sign < 0) for value in pair]
                    for side in range(2):
                        if spread[0][0][side] is None:
                            continue
                        pieces = [(spread[0][spin][side], spread[1][spin][side]) for spin in range(2)]
                        for spin in range(4):
                            base = totals[spin][0][side], totals[spin][1][side]
                            if spin < 2:
                                total = add_phase(base, pieces[spin], 0, 1)
                            else:
                                source, power = LOWER[mu][spin - 2]
                                total = add_phase(base, pieces[source], power, sign)
                            totals[spin][0][side], totals[spin][1][side] = total
                for spin in range(4):
                    for part in range(2):
                        for side in range(2):
                            hops[hop_rows(part, spin, row, side), :] = totals[spin][part][side]
        return carry

    lax.fori_loop(0, SWEEPS, body, 0)

    residual = [HOPPING * hops[pl.ds(r, 48, stride=8), :] for r in range(8)]
    rows = jnp.concatenate(residual, axis=0).astype(BF16)
    mine = me["xy"]

    def parcel(owner):
        return pltpu.make_async_remote_copy(
            src_ref=parcels.at[owner],
            dst_ref=arrived.at[mine],
            send_sem=parcel_send.at[owner],
            recv_sem=parcel_recv.at[mine],
            device_id={"xy": owner},
            device_id_type=MESH,
        )

    placed = jnp.dot(rows, placing[...], preferred_element_type=F32)
    lane = lax.broadcasted_iota(jnp.int32, (48, 128), 1) // 16
    flags = {step: jnp.where((lane & step) != 0, 1.0, 0.0).astype(BF16) for step in (1, 2, 4)}
    for part in range(slots // 8):
        parts = [placed[r * 48:(r + 1) * 48, part * 128:(part + 1) * 128].astype(BF16) for r in range(8)]
        for step in (4, 2, 1):
            for r in range(8):
                if r & step:
                    continue
                first, second = parts[r], parts[r + step]
                odd = flags[step] > 0
                parts[r] = jnp.where(odd, roll(second, step * 16, 1), first)
                parts[r + step] = jnp.where(odd, second, roll(first, -step * 16, 1))
        for r in range(8):
            slot = part * 8 + r
            parcels[slot // MOST, slot % MOST] = parts[r]
    for turn in sorted(range(1, groups), key=lambda o: -min(o, groups - o)):
        parcel(lax.rem(mine + turn, groups)).start()

    for sweep in range(SWEEPS):
        for order, (mu, axis) in enumerate(CROSSING):
            message(sweep, 2 * order, axis, -1).wait_send()
            message(sweep, 2 * order + 1, axis, 1).wait_send()
    loads[3].wait()

    def contract(index, carry):
        pair = index // 2
        away = jnp.where(pair == 2, groups // 2 - 1, jnp.where(pair == 3, groups // 2 - 2, pair))
        chip = lax.rem(mine // 2 + away, groups // 2)
        source = chip * 2 + lax.rem(mine + index, 2)

        @pl.when(index > 0)
        def _():
            pltpu.make_async_remote_copy(
                src_ref=parcels.at[source],
                dst_ref=arrived.at[source],
                send_sem=parcel_send.at[source],
                recv_sem=parcel_recv.at[source],
                device_id={"xy": source},
                device_id_type=MESH,
            ).wait_recv()

        @pl.when(index == 0)
        def _():
            arrived[mine] = parcels[mine]

        for m in range(MOST):
            slot = source * MOST + m
            tile = arrived[source, m].astype(F32).reshape(6, 8, 128)
            turned = jnp.concatenate([tile[3:], -tile[:3]], axis=0)
            for v in range(NV):
                vector = near[slot * NV + v].astype(F32).reshape(6, 8, 128)
                for part, other in enumerate((tile, turned)):
                    total = jnp.sum(jnp.sum(vector * other, axis=0), axis=1, keepdims=True)
                    sums[v * 2 + part] = jnp.where(lane8 == slot, total, sums[v * 2 + part])
        return carry

    lax.fori_loop(0, groups, contract, 0)
    for turn in range(1, groups):
        parcel(lax.rem(mine + turn, groups)).wait_send()


def finish(smooth, sums, smoothed, coarse, staged, sems):
    first = pltpu.make_async_copy(smooth, smoothed, sems.at[0])
    first.start()
    slots = coarse.shape[-1]
    total = sums[...]
    total = total + roll(total, 4, 1)
    total = total + roll(total, -1, 1)
    total = total.reshape(NV, 2, 8, 128)
    for chirality in range(2):
        staged[chirality] = total[:, :, 2 * chirality, :slots]
    second = pltpu.make_async_copy(staged, coarse, sems.at[1])
    second.start()
    first.wait()
    second.wait()


def shards(right_side, links, clover_inverse, near_null, owners):
    groups = lax.axis_size("xy")
    slots = groups * MOST
    near = jnp.transpose(near_null[0, 0, 0], (0, 1, 2, 4, 3, 5)).reshape(slots, NV, 2, 3, 4, 2, 128)
    near = jnp.transpose(near, (0, 1, 2, 3, 5, 4, 6)).reshape(slots * NV, 48, 128)
    anywhere = pl.BlockSpec(memory_space=pl.ANY)
    vmem = pltpu.VMEM
    inside = pl.BlockSpec(memory_space=vmem)
    operands = [
        pltpu.with_memory_space_constraint(value, pltpu.HBM)
        for value in (
            right_side.reshape(24, 2, 8, 128),
            links.reshape(4, 2, 9, 16, 128),
            clover_inverse.reshape(2, 2, 36, 16, 128),
            near,
            owners.reshape(-1),
        )
    ]
    smooth, sums = pl.pallas_call(
        kernel,
        out_shape=(vmem((24, 2, 8, 128), F32), vmem((NV * 2, 8, 128), F32)),
        in_specs=[anywhere] * 5,
        out_specs=(inside, inside),
        scratch_shapes=[
            vmem((24, 2, 8, 128), F32),
            vmem((4, 2, 9, 16, 128), BF16),
            vmem((2, 2, 36, 16, 128), BF16),
            vmem((slots * NV, 48, 128), BF16),
            pltpu.SMEM((AGGS,), jnp.int32),
            vmem((4, 2, 9, 2, 8, 128), F32),
            vmem((3, 2, 9, 8, 128), F32),
            vmem((24, 2, 8, 128), F32),
            vmem((384, 128), F32),
            vmem((SWEEPS, 6, 6, 8, 128), F32),
            vmem((SWEEPS, 6, 6, 8, 128), F32),
            vmem((128, slots * 16), BF16),
            vmem((groups, MOST, 48, 128), BF16),
            vmem((groups, MOST, 48, 128), BF16),
            pltpu.SemaphoreType.DMA((5,)),
            pltpu.SemaphoreType.DMA((SWEEPS, 6)),
            pltpu.SemaphoreType.DMA((SWEEPS, 6)),
            pltpu.SemaphoreType.DMA((groups,)),
            pltpu.SemaphoreType.DMA((groups,)),
        ],
        compiler_params=pltpu.CompilerParams(
            collective_id=0, has_side_effects=True, vmem_limit_bytes=32 * 1024 * 1024
        ),
        name="smooth_and_restrict",
    )(*operands)
    smoothed, coarse = pl.pallas_call(
        finish,
        out_shape=(
            jax.ShapeDtypeStruct((24, 2, 8, 128), F32),
            jax.ShapeDtypeStruct((2, NV, 2, slots), F32),
        ),
        in_specs=[anywhere, inside],
        out_specs=(anywhere, anywhere),
        scratch_shapes=[vmem((2, NV, 2, slots), F32), pltpu.SemaphoreType.DMA((2,))],
        compiler_params=pltpu.CompilerParams(vmem_limit_bytes=32 * 1024 * 1024),
        name="finish",
    )(smooth, sums)
    coarse = jnp.transpose(coarse, (3, 0, 2, 1))[None, None, None]
    return smoothed.reshape(2, 4, 3, 4, 4, 128), coarse


def solution(mesh):
    placed = (
        P(None, None, None, "ta", "gz", "xy"),
        P(None, None, None, None, "ta", "gz", "xy"),
        P(None, None, None, None, "ta", "gz", "xy"),
        P("ta", "gz", "xy", None, None, None, None, None, None),
        P("ta", "gz", "xy", None),
    )
    return jax.shard_map(
        shards,
        mesh=mesh,
        in_specs=placed,
        out_specs=(
            P(None, None, None, "ta", "gz", "xy"),
            P("ta", "gz", "xy", None, None, None, None),
        ),
        check_vma=False,
    )
```
